128 devices in a mesh: outer: 16 (over z_lo, y, core), inner: 8 (over x, z_hi).
Axes of the slice: x: 4, y: 4, z: 4 (z_hi: 2, z_lo: 2; z = z_hi * 2 + z_lo), core: 2. Of those that a mesh axis runs over, the one named last changes fastest.
Arguments:
- tokens: bfloat16 [32768, 14848], P(('outer', 'inner')), may hold values from -24 to 24
- cotangent: bfloat16 [32768, 512], P(('outer', 'inner')), may hold values from -6 to 6
- lengths: int32 [8], replicated, may hold values from 1 to 4096
- frozen: bfloat16 [14848, 512], P(('outer', 'inner')), may hold values from -0.046875 to 0.046875
- down_weight: bfloat16 [14848, 64], P(('outer', 'inner')), may hold values from -0.046875 to 0.046875
- up_weight: bfloat16 [64, 512], replicated, may hold values from -0.75 to 0.75
Outputs:
- keys: bfloat16 [32768, 512], P(('outer', 'inner'))
- input_gradient: bfloat16 [32768, 14848], P(('outer', 'inner'))
- down_gradient: float32 [14848, 64], P(('outer', 'inner'))
- up_gradient: float32 [64, 512], replicated
The draws below stay inside these ranges and needn't reach their ends.
All inputs are finite; a program needn't handle non-finite values.
Results may differ from the reference program's by a relative error of at most 0.0046.
Values may be sent and summed in bfloat16 or wider, within the bound.
A program may use at most 128 MiB of HBM per device.

```python
import jax
import jax.numpy as jnp
from jax import lax

D = 14848
KV = 512
RANK = 64
SEQ_LEN = 4096
TOKENS = 32768
SEQS = 8


def plant(drawn, key, low, high):
    spot = [jax.random.randint(jax.random.fold_in(key, axis), (), 0, length) for axis, length in enumerate(drawn.shape)]
    widest = drawn.shape.index(max(drawn.shape))
    beside = spot[:widest] + [(spot[widest] + 1) % drawn.shape[widest]] + spot[widest + 1:]
    return drawn.at[tuple(spot)].set(low).at[tuple(beside)].set(high)


def raised(values, own_key, source, target, blocks, factor):
    def block_of(position):
        return (jnp.arange(values.shape[position]) // (values.shape[position] // blocks)).reshape((-1,) + (1,) * (values.ndim - 1 - position))

    first = jax.random.permutation(own_key, blocks)[block_of(target)]
    far = (block_of(target) + blocks // 2) % blocks
    return jnp.where((block_of(source) == first) | (block_of(source) == far), factor * values, values)


def steps_of(stream_key, dims, split, least, largest):
    factor_of, own = 1.0, jax.random.fold_in(stream_key, 6)
    for dim, blocks in split:
        draws = jnp.exp(jax.random.uniform(jax.random.fold_in(own, dim), (blocks,), jnp.float32, least / len(split), largest / len(split)))
        factor_of = factor_of * jnp.repeat(draws, dims[dim] // blocks).reshape([-1 if axis == dim else 1 for axis in range(len(dims))])
    return factor_of


def bell_draw(rng, dims, width, bound, cuts=(), kind=jnp.bfloat16):
    level = steps_of(rng, dims, cuts, -0.22, 0.18) if cuts else 1.0
    entries = jax.random.normal(rng, dims, jnp.float32) * width * level
    return jnp.minimum(jnp.maximum(entries, -bound), bound).astype(kind)


def heavy_noise(own_key, shape, width, reach, pieces, heavy, kind=jnp.bfloat16):
    values = width * jax.random.normal(own_key, shape, jnp.float32)
    if pieces:
        values = values * steps_of(own_key, shape, pieces, -0.22, 0.18)
    return jnp.clip(raised(values, jax.random.fold_in(own_key, 3), *heavy), -reach, reach).astype(kind)


def setup_inputs(seed: int = 0) -> dict:
    key_of = jax.random.split(jax.random.key(seed), 7)
    tokens = heavy_noise(key_of[0], (TOKENS, D), 1.0, 24.0, ((0, 128),), (0, 1, 128, 5.5))
    cotangent = bell_draw(key_of[1], (TOKENS, KV), 1.0, 6.0, ((0, 128),))
    lengths = plant(jax.random.randint(key_of[2], (SEQS,), 1, SEQ_LEN + 1), jax.random.fold_in(key_of[2], 1), 1, SEQ_LEN).astype(jnp.int32)
    frozen = bell_draw(key_of[3], (D, KV), D ** -0.5, 0.046875, ((0, 128),))
    down_weight = bell_draw(key_of[4], (D, RANK), D ** -0.5, 0.046875, ((0, 128),))
    up_weight = bell_draw(key_of[5], (RANK, KV), RANK ** -0.5, 0.75)
    return {"tokens": tokens, "cotangent": cotangent, "lengths": lengths, "frozen": frozen, "down_weight": down_weight, "up_weight": up_weight}


adapter_scale = 2.0


def reference(tokens, cotangent, lengths, frozen, down_weight, up_weight):
    token_blocks = tokens.reshape(SEQS, SEQ_LEN, D)
    grad_blocks = cotangent.reshape(SEQS, SEQ_LEN, KV)

    def per_sequence(item):
        token_block, incoming, length = item
        live = (jnp.arange(SEQ_LEN, dtype=jnp.int32) < length).astype(jnp.bfloat16)
        reduced_rank_output = jnp.dot(token_block, down_weight, preferred_element_type=jnp.float32).astype(jnp.bfloat16)
        keys = jnp.dot(token_block, frozen, preferred_element_type=jnp.float32) + adapter_scale * jnp.dot(reduced_rank_output, up_weight, preferred_element_type=jnp.float32)
        masked_tokens = incoming * live[:, None]
        expanded_output = jnp.dot(masked_tokens, up_weight.T, preferred_element_type=jnp.float32).astype(jnp.bfloat16)
        input_gradient = jnp.dot(masked_tokens, frozen.T, preferred_element_type=jnp.float32) + adapter_scale * jnp.dot(expanded_output, down_weight.T, preferred_element_type=jnp.float32)
        down_gradient = adapter_scale * jnp.dot(token_block.T, expanded_output, preferred_element_type=jnp.float32)
        up_gradient = adapter_scale * jnp.dot(reduced_rank_output.T, masked_tokens, preferred_element_type=jnp.float32)
        return keys.astype(jnp.bfloat16), input_gradient.astype(jnp.bfloat16), down_gradient, up_gradient

    keys, input_gradient, down_gradient, up_gradient = lax.map(per_sequence, (token_blocks, grad_blocks, lengths))
    return (keys.reshape(TOKENS, KV), input_gradient.reshape(TOKENS, D), jnp.sum(down_gradient, axis=0), jnp.sum(up_gradient, axis=0))
```

```python
import jax
import jax.numpy as jnp
from jax import lax
from jax.experimental import pallas as pl
from jax.experimental.pallas import tpu as pltpu
from jax.sharding import PartitionSpec as P

MESH = pl.DeviceIdType.MESH
F32, BF16 = jnp.float32, jnp.bfloat16

D, KV, RANK, SEQ_LEN, ROWS, OWN = 14848, 512, 64, 4096, 256, 116
QUAD = 4 * OWN
STEP = 3712
adapter_scale = 2.0

STREAMS = (
    ("down", "zxy", 0, 64),
    ("w", "xyz", 0, 176),
    ("w", "yzx", 176, 176),
    ("w", "zxy", 352, 112),
)
SUMS = (("xyz", 0, 24, 8), ("yzx", 24, 24, 16), ("zxy", 48, 16, 8))
NSEM = 40
ALL = slice(None)


def comm_kernel(
    lengths, tokens_hbm, cot, frozen, down_t, up,
    w, dt, tokens, masked_out, raised_out, lowered_out, dgrad, ugrad,
    stage, quad, dt_raw, g, r, x0, xa, xb, xl, xr, y2, y3, v0, v1, v2, v3, v5,
    load_sem, quad_s, quad_r, ag_s, ag_r, sib_s, sib_r, rs_s, rs_r, up_s, up_r,
):
    outer, inner = lax.axis_index("outer"), lax.axis_index("inner")
    core = outer % 2
    me = {"x": inner // 2, "y": (outer // 2) % 4, "z": (inner % 2) * 2 + outer // 8}

    def device(core=core, **at):
        c = dict(me, **at)
        return ((c["z"] % 2) * 8 + c["y"] * 2 + core, c["x"] * 2 + c["z"] // 2)

    def step(axis, by):
        return (me[axis] + by) % 4

    sibling = device(core=1 - core)
    pending = []

    def send(src, dst, s, r_, to):
        copy = pltpu.make_async_remote_copy(
            src_ref=src, dst_ref=dst, send_sem=s, recv_sem=r_, device_id=to, device_id_type=MESH
        )
        copy.start()
        return copy

    load = pltpu.make_async_copy(tokens_hbm, tokens, load_sem)
    load.start()

    barrier = pltpu.get_barrier_semaphore()
    peers = [device(**{a: step(a, by)}) for a in "xyz" for by in (1, 2, 3)]
    xq = me["x"] + 1 - 2 * (me["x"] % 2)
    zq = step("z", 2)
    peers += [sibling, device(x=xq, z=zq)]
    for peer in peers:
        pl.semaphore_signal(barrier, inc=1, device_id=peer, device_id_type=MESH)

    kx, kz = me["x"] % 2, me["z"] // 2
    mine = kx * 2 + kz
    stage[...] = jnp.zeros_like(stage)
    for k in range(4):
        stage[k, 0:OWN, :] = frozen[:, 128 * k : 128 * (k + 1)]
    at_home = (me["z"] % 2, me["y"], core, me["x"], me["z"] // 2)
    dt_raw[at_home] = jnp.concatenate([down_t[...], jnp.zeros((RANK, 128 - OWN), BF16)], axis=1)

    pl.semaphore_wait(barrier, len(peers))

    quad_copies = []
    for n, (dx, dz) in enumerate(((1, 0), (0, 1), (1, 1))):
        tx, tz = (kx + dx) % 2, (kz + dz) % 2
        to = device(x=xq if dx else me["x"], z=zq if dz else me["z"])
        quad_copies.append(
            send(stage.at[tx * 2 + tz], quad.at[mine], quad_s.at[n], quad_r.at[n], to)
        )
    quad[mine] = stage[mine]

    first = (outer % 2 * 8 + inner) * ROWS
    length = lengths[outer // 2]
    position = first + lax.broadcasted_iota(jnp.int32, (ROWS, KV), 0)
    live = jnp.where(position < length, 1.0, 0.0).astype(BF16)
    masked = cot[...] * live
    masked_out[...] = masked
    contract = (((1,), (1,)), ((), ()))
    raised = lax.dot_general(masked, up[...], contract, preferred_element_type=F32).astype(BF16)
    raised2 = raised * jnp.asarray(adapter_scale, BF16)
    raised_out[...] = raised2
    raised2_t = raised2.astype(F32).T.astype(BF16)

    def at_of(kind, at, r0, n):
        x, y, z, c = at["x"], at["y"], at["z"], at["core"]
        whole = lambda v: isinstance(v, slice)
        zhi, zlo = (ALL, ALL) if whole(z) else (z // 2, z % 2)
        rows = pl.ds(r0, n)
        if kind == "down":
            return dt_raw.at[zlo, y, c, x, zhi, rows, :]
        xhi, xlo = (ALL, ALL) if whole(x) else (x // 2, x % 2)
        return w.at[xlo, zhi, zlo, y, c, xhi, rows, :]

    streams = []

    class Stream:
        def __init__(self, n):
            self.n = n
            self.kind, (self.a, self.b, self.c), self.r0, self.rows = STREAMS[n]
            self.cut = self.rows // 32 * 16
            self.copies = {}
            self.sem = 0
            self.sib_sem = 0
            self.sib_copies = []

        def ref(self, at, part=None):
            r0, rows = self.r0, self.rows
            if part == 0:
                rows = self.cut
            elif part == 1:
                r0, rows = r0 + self.cut, rows - self.cut
            return at_of(self.kind, {**me, "core": core, **at}, r0, rows)

        def go(self, key, axis, by, at, part=None):
            ref = self.ref(at, part)
            copy = send(
                ref, ref, ag_s.at[self.n, self.sem], ag_r.at[self.n, self.sem],
                device(**{axis: step(axis, by)}),
            )
            self.sem += 1
            self.copies[key] = copy

        def sib(self, at):
            ref = self.ref(at)
            self.sib_copies.append(
                send(ref, ref, sib_s.at[self.n, self.sib_sem], sib_r.at[self.n, self.sib_sem], sibling)
            )
            self.sib_sem += 1

        def open(self, name, axis, at):
            self.go(name + "R", axis, 1, {**at, axis: me[axis]})
            self.go(name + "L", axis, -1, {**at, axis: me[axis]})

        def forward(self, name, axis, at):
            self.copies[name + "R"].wait_recv()
            self.go(name + "r", axis, 1, {**at, axis: step(axis, -1)}, 0)
            self.copies[name + "L"].wait_recv()
            self.go(name + "l", axis, -1, {**at, axis: step(axis, 1)}, 1)

        def close(self, name):
            self.copies[name + "r"].wait_recv()
            self.copies[name + "l"].wait_recv()

        def open1(self):
            self.open("1", self.a, {})

        def forward1(self):
            self.forward("1", self.a, {})

        def close1(self):
            self.close("1")
            at = {self.a: ALL}
            self.open("2", self.b, at)
            self.sib(at)

        def sub(self, j):
            return {self.a: ALL, self.b: step(self.b, (0, -1, 1, 2)[j])}

        def open3(self, j):
            self.open(f"3{j}", self.c, self.sub(j))

        def forward2(self):
            self.forward("2", self.b, {self.a: ALL})
            self.sib(self.sub(1))
            self.sib(self.sub(2))

        def close2(self):
            self.close("2")
            self.sib(self.sub(3))

        def forward3(self, j):
            self.forward(f"3{j}", self.c, self.sub(j))
            self.sib({**self.sub(j), self.c: step(self.c, -1)})
            self.sib({**self.sub(j), self.c: step(self.c, 1)})

        def close3(self, j):
            self.close(f"3{j}")
            self.sib({**self.sub(j), self.c: step(self.c, 2)})

        def end_sib(self):
            for copy in self.sib_copies:
                copy.wait_recv()

        def end(self):
            for copy in list(self.copies.values()) + self.sib_copies:
                copy.wait_send()

    streams = [Stream(n) for n in range(len(STREAMS))]

    x0_copies = []

    def owners(c):
        load_once(c)
        for n in range(0, STEP, 256):
            m = min(256, STEP - n)
            g[:, n : n + m] = jnp.dot(
                raised2_t, tokens[:, STEP * c + n : STEP * c + n + m], preferred_element_type=F32
            )
        for i in range(32):
            o, x, zhi = i // 8, i // 2 % 4, i % 2
            piece = g[:, OWN * i : OWN * (i + 1)]
            r[c // 2, 2 * (c % 2) + o // 2, o % 2, x, zhi, :, 0:OWN] = piece
            r[c // 2, 2 * (c % 2) + o // 2, o % 2, x, zhi, :, OWN:128] = jnp.zeros((RANK, 128 - OWN), F32)
        zlo, y = c // 2, pl.ds(2 * (c % 2), 2)
        x0_copies.append(
            send(r.at[zlo, y, 1 - core], x0.at[zlo, y], rs_s.at[0, c], rs_r.at[0, c], sibling)
        )

    def load_once(c):
        if c == 0:
            load.wait()

    def add_sibling(c):
        x0_copies[c].wait_recv()
        for y in range(2 * (c % 2), 2 * (c % 2) + 2):
            for x in range(4):
                r[c // 2, y, core, x] = r[c // 2, y, core, x] + x0[c // 2, y, x]

    def r_at(at, r0, n):
        z = at["z"]
        zhi, zlo = (ALL, ALL) if isinstance(z, slice) else (z // 2, z % 2)
        return r.at[zlo, at["y"], core, at["x"], zhi, pl.ds(r0, n), :]

    class Sum:
        def __init__(self, n):
            self.n = n
            (self.a, self.b, self.c), self.r0, self.rows, self.cut = SUMS[n]
            self.free = {self.a: ALL, self.b: ALL, self.c: ALL}
            self.sends = []

        def go(self, src, dst, k, axis, by):
            copy = send(src, dst, rs_s.at[1 + self.n, k], rs_r.at[1 + self.n, k], device(**{axis: step(axis, by)}))
            self.sends.append(copy)
            return copy

        def at(self, by, half=None):
            r0, rows = self.r0, self.rows
            if half == 0:
                rows = self.cut
            elif half == 1:
                r0, rows = r0 + self.cut, rows - self.cut
            return r_at({**self.free, self.a: step(self.a, by)}, r0, rows)

        def first(self):
            self.ca = self.go(self.at(2, 0), xa[self.n], 0, self.a, 1)
            self.cb = self.go(self.at(2, 1), xb[self.n], 1, self.a, -1)

        def second(self):
            self.ca.wait_recv()
            ref = self.at(1, 0)
            ref[...] = ref[...] + xa[self.n][...]
            self.cl = self.go(self.at(1), xl[self.n], 2, self.a, 1)
            self.cb.wait_recv()
            ref = self.at(-1, 1)
            ref[...] = ref[...] + xb[self.n][...]
            self.cr = self.go(self.at(-1), xr[self.n], 3, self.a, -1)

        def third(self):
            self.cl.wait_recv()
            self.cr.wait_recv()
            ref = self.at(0)
            ref[...] = ref[...] + xl[self.n][...] + xr[self.n][...]
            self.k = []
            for j, by in enumerate((1, -1, 2)):
                src = r_at({**self.free, self.a: me[self.a], self.b: step(self.b, by)}, self.r0, self.rows)
                self.k.append(self.go(src, y2[self.n].at[j], 4 + j, self.b, by))

        def fourth(self):
            for copy in self.k:
                copy.wait_recv()
            ref = r_at({**me, self.c: ALL}, self.r0, self.rows)
            ref[...] = ref[...] + y2[self.n][0] + y2[self.n][1] + y2[self.n][2]
            self.k = []
            for j, by in enumerate((1, -1, 2)):
                src = r_at({**me, self.c: step(self.c, by)}, self.r0, self.rows)
                self.k.append(self.go(src, y3[self.n].at[j], 7 + j, self.c, by))

        def fifth(self):
            for copy in self.k:
                copy.wait_recv()
            own = r_at(me, self.r0, self.rows)
            total = own[...] + y3[self.n][0] + y3[self.n][1] + y3[self.n][2]
            dgrad[self.r0 : self.r0 + self.rows, :] = total[:, 0:OWN]

        def end(self):
            for copy in self.sends:
                copy.wait_send()

    sums = [Sum(n) for n in range(3)]

    up_copies = []

    def up_send(src, dst, k, to):
        copy = send(src, dst, up_s.at[k], up_r.at[k], to)
        up_copies.append(copy)
        return copy

    def rows_at(c, z=None):
        return pl.ds(pl.multiple_of(c * 32, 8), 32) if z is None else pl.ds(pl.multiple_of(c * 32 + z * 8, 8), 8)

    state = {}

    def lowered_and_up():
        def chunk(c, carry):
            for i in range(32):
                o, x, zhi = i // 8, i // 2 % 4, i % 2
                piece = dt_raw[c // 2, 2 * (c % 2) + o // 2, o % 2, x, zhi]
                dt[:, OWN * i + STEP * c : OWN * (i + 1) + STEP * c] = piece[:, 0:OWN]
            return carry

        for c in range(4):
            chunk(c, 0)
        total = jnp.zeros((ROWS, RANK), F32)
        for c in range(29):
            total += lax.dot_general(
                tokens[:, 512 * c : 512 * (c + 1)], dt[:, 512 * c : 512 * (c + 1)], contract,
                preferred_element_type=F32,
            )
        lowered2 = total.astype(BF16) * jnp.asarray(adapter_scale, BF16)
        lowered_out[...] = lowered2
        lowered2_t = lowered2.astype(F32).T.astype(BF16)
        ugrad[...] = jnp.dot(lowered2_t, masked_out[...], preferred_element_type=F32)
        state["k"] = [up_send(ugrad.at[rows_at(1 - core)], v0, 0, sibling)]

    def wait_up():
        for copy in state["k"]:
            copy.wait_recv()

    def up_z():
        wait_up()
        own = rows_at(core)
        v0[...] = v0[...] + ugrad[own, :]
        state["k"] = []
        for j, by in enumerate((1, 2, 3)):
            z = step("z", by)
            src = v0.at[pl.ds(pl.multiple_of(z * 8, 8), 8)]
            state["k"].append(up_send(src, v1.at[j], 1 + j, device(z=z)))

    def up_x():
        wait_up()
        own = v0[pl.ds(pl.multiple_of(me["z"] * 8, 8), 8), :]
        v2[me["x"]] = own + v1[0] + v1[1] + v1[2]
        state["k"] = [
            up_send(v2.at[me["x"]], v2.at[me["x"]], 4 + j, device(x=step("x", by)))
            for j, by in enumerate((1, 2, 3))
        ]

    def up_y():
        wait_up()
        v3[me["y"]] = v2[0] + v2[1] + v2[2] + v2[3]
        state["k"] = [
            up_send(v3.at[me["y"]], v3.at[me["y"]], 7 + j, device(y=step("y", by)))
            for j, by in enumerate((1, 2, 3))
        ]

    def up_gather():
        wait_up()
        own = rows_at(core, me["z"])
        ugrad[own, :] = v3[0] + v3[1] + v3[2] + v3[3]
        ref = ugrad.at[own]
        state["k"] = [up_send(ref, ref, 10 + j, device(z=step("z", by))) for j, by in enumerate((1, 2, 3))]

    def up_pair():
        wait_up()
        state["k"] = [up_send(ugrad.at[rows_at(core)], v5, 13, sibling)]

    owners(0)
    for copy in quad_copies:
        copy.wait_recv()
    piece = jnp.concatenate([quad[k, 0:OWN, :].astype(F32) for k in range(4)], axis=0).astype(BF16)
    w[kx, kz, me["z"] % 2, me["y"], core, me["x"] // 2] = piece
    for s in streams:
        s.open1()
    owners(1)
    for s in streams:
        s.forward1()
    owners(2)
    for s in streams:
        s.close1()
    for s in streams:
        s.open3(0)
    owners(3)
    for s in streams:
        s.forward2()
    for c in range(4):
        add_sibling(c)
    for s in sums:
        s.first()
    for s in streams:
        s.open3(1)
        s.open3(2)
    for s in streams:
        s.close2()
    for s in sums:
        s.second()
    for s in streams:
        s.open3(3)
    for s in streams:
        s.forward3(0)
    for s in sums:
        s.third()
    for s in streams:
        s.forward3(1)
    for s in sums:
        s.fourth()
    for s in streams:
        s.forward3(2)
    for s in sums:
        s.fifth()
    down = streams[0]
    down.forward3(3)
    for j in range(4):
        down.close3(j)
    down.end_sib()
    lowered_and_up()
    for s in streams[1:]:
        s.forward3(3)
    up_z()
    for s in streams[1:]:
        s.close3(0)
    up_x()
    for s in streams[1:]:
        s.close3(1)
    up_y()
    for s in streams[1:]:
        s.close3(2)
    up_gather()
    for s in streams[1:]:
        s.close3(3)
    up_pair()
    for s in streams[1:]:
        s.end_sib()
    wait_up()
    up_copies[0].wait_send()
    ugrad[rows_at(1 - core), :] = v5[...]
    for s in streams:
        s.end()
    for s in sums:
        s.end()
    for copy in quad_copies + x0_copies + up_copies[1:]:
        copy.wait_send()


def product_kernel(
    up, w, dt, tokens, masked, raised2, lowered2, dgrad_in, ugrad_in,
    keys, ig_hbm, dgrad, ugrad,
    ig, store_sem,
):
    width = 512
    steps = D // width

    def store(c):
        at = pl.ds(pl.multiple_of(c * width, 128), width)
        return pltpu.make_async_copy(ig.at[:, at], ig_hbm.at[:, at], store_sem.at[c])

    dgrad[...] = dgrad_in[...]
    ugrad[...] = ugrad_in[...]
    contract = (((1,), (1,)), ((), ()))

    def body(c, total):
        at = pl.ds(pl.multiple_of(c * width, 128), width)
        wc = jnp.concatenate([w[k, at, :] for k in range(4)], axis=1)
        out = lax.dot_general(masked[...], wc, contract, preferred_element_type=F32)
        out += jnp.dot(raised2[...], dt[:, at], preferred_element_type=F32)
        ig[:, at] = out.astype(BF16)
        store(c).start()
        return total + jnp.dot(tokens[:, at], wc, preferred_element_type=F32)

    total = jnp.dot(lowered2[...], up[...], preferred_element_type=F32)
    total = lax.fori_loop(0, steps, body, total)
    keys[...] = total.astype(BF16)
    for c in range(steps):
        store(c).wait()


def on_device(tokens, cotangent, lengths, frozen, down_weight, up_weight):
    vmem = pl.BlockSpec(memory_space=pltpu.VMEM)
    anywhere = pl.BlockSpec(memory_space=pl.ANY)
    in_hbm = lambda array: pltpu.with_memory_space_constraint(array, pltpu.HBM)
    down_t = down_weight.T
    axis_dims = {"x": (4,), "y": (4,), "z": (2, 2)}

    def free_dims(first):
        dims = []
        for name, axis in (("z", 2), ("y", 4), ("x", 4), ("z", 2)):
            if name != first:
                dims.append(axis)
        return tuple(dims)

    def buffers(shape):
        return [pltpu.VMEM(shape(n), F32) for n in range(3)]

    def cdims(axis):
        return (2, 2) if axis == "z" else (4,)

    scratch = [
        pltpu.VMEM((4, 128, 128), BF16),
        pltpu.VMEM((4, 128, 128), BF16),
        pltpu.VMEM((2, 4, 2, 4, 2, RANK, 128), BF16),
        pltpu.VMEM((RANK, STEP), F32),
        pltpu.VMEM((2, 4, 2, 4, 2, RANK, 128), F32),
        pltpu.VMEM((2, 4, 4, 2, RANK, 128), F32),
        buffers(lambda n: free_dims(SUMS[n][0][0]) + (SUMS[n][3], 128)),
        buffers(lambda n: free_dims(SUMS[n][0][0]) + (SUMS[n][2] - SUMS[n][3], 128)),
        buffers(lambda n: free_dims(SUMS[n][0][0]) + (SUMS[n][2], 128)),
        buffers(lambda n: free_dims(SUMS[n][0][0]) + (SUMS[n][2], 128)),
        buffers(lambda n: (3,) + cdims(SUMS[n][0][2]) + (SUMS[n][2], 128)),
        buffers(lambda n: (3, SUMS[n][2], 128)),
        pltpu.VMEM((32, KV), F32),
        pltpu.VMEM((3, 8, KV), F32),
        pltpu.VMEM((4, 8, KV), F32),
        pltpu.VMEM((4, 8, KV), F32),
        pltpu.VMEM((32, KV), F32),
        pltpu.SemaphoreType.DMA,
        pltpu.SemaphoreType.DMA((3,)),
        pltpu.SemaphoreType.DMA((3,)),
        pltpu.SemaphoreType.DMA((4, NSEM)),
        pltpu.SemaphoreType.DMA((4, NSEM)),
        pltpu.SemaphoreType.DMA((4, 16)),
        pltpu.SemaphoreType.DMA((4, 16)),
        pltpu.SemaphoreType.DMA((4, 10)),
        pltpu.SemaphoreType.DMA((4, 10)),
        pltpu.SemaphoreType.DMA((14,)),
        pltpu.SemaphoreType.DMA((14,)),
    ]
    gathered = pl.pallas_call(
        comm_kernel,
        out_shape=(
            pltpu.VMEM((2, 2, 2, 4, 2, 2, QUAD, 128), BF16),
            pltpu.VMEM((RANK, D), BF16),
            pltpu.VMEM((ROWS, D), BF16),
            pltpu.VMEM((ROWS, KV), BF16),
            pltpu.VMEM((ROWS, RANK), BF16),
            pltpu.VMEM((ROWS, RANK), BF16),
            pltpu.VMEM((RANK, OWN), F32),
            pltpu.VMEM((RANK, KV), F32),
        ),
        in_specs=[pl.BlockSpec(memory_space=pltpu.SMEM), anywhere] + [vmem] * 4,
        out_specs=(vmem,) * 8,
        scratch_shapes=scratch,
        compiler_params=pltpu.CompilerParams(
            collective_id=0, has_side_effects=True, vmem_limit_bytes=20 * 1024 * 1024
        ),
        name="gather_and_sum",
    )(lengths, in_hbm(tokens), cotangent, frozen, down_t, up_weight)
    gathered = (gathered[0].reshape(4, D, 128),) + tuple(gathered[1:])
    gathered = [pltpu.with_memory_space_constraint(part, pltpu.VMEM) for part in gathered]
    keys, ig, dgrad, ugrad = pl.pallas_call(
        product_kernel,
        out_shape=(
            jax.ShapeDtypeStruct((ROWS, KV), BF16),
            jax.ShapeDtypeStruct((ROWS, D), BF16),
            jax.ShapeDtypeStruct((RANK, OWN), F32),
            jax.ShapeDtypeStruct((RANK, KV), F32),
        ),
        in_specs=[vmem] * 9,
        out_specs=(vmem, anywhere, vmem, vmem),
        scratch_shapes=[
            pltpu.VMEM((ROWS, D), BF16),
            pltpu.SemaphoreType.DMA((D // 512,)),
        ],
        compiler_params=pltpu.CompilerParams(vmem_limit_bytes=16 * 1024 * 1024),
        name="products",
    )(up_weight, *gathered)
    return keys, ig, dgrad.T, ugrad


def solution(mesh):
    return jax.shard_map(
        on_device,
        mesh=mesh,
        in_specs=(
            P(("outer", "inner"), None),
            P(("outer", "inner"), None),
            P(),
            P(("outer", "inner"), None),
            P(("outer", "inner"), None),
            P(),
        ),
        out_specs=(
            P(("outer", "inner"), None),
            P(("outer", "inner"), None),
            P(("outer", "inner"), None),
            P(),
        ),
        check_vma=False,
    )
```

```python
import jax
import jax.numpy as jnp
from jax import lax
from jax.experimental import pallas as pl
from jax.experimental.pallas import tpu as pltpu
from jax.sharding import PartitionSpec as P

MESH = pl.DeviceIdType.MESH
F32, BF16 = jnp.float32, jnp.bfloat16

D, KV, RANK, SEQ_LEN, ROWS, OWN = 14848, 512, 64, 4096, 256, 116
QUAD = 4 * OWN
STEP = 3712
adapter_scale = 2.0

STREAMS = {
    "D": ("down", "yzx", 0, 64),
    "Z": ("w", "xyz", 0, 192),
    "X": ("w", "zyx", 192, 128),
    "Y": ("w", "xzy", 320, 144),
}
SUMS = (("xyz", 0, 24, 8), ("yzx", 24, 24, 16), ("zxy", 48, 16, 8))
ALL = slice(None)


def comm_kernel(
    lengths_hbm, tokens_hbm, cot_hbm, frozen_hbm, down_hbm, up_hbm,
    ig, keys, dgrad, ugrad,
    w, dt, tokens, lengths, cot, frozen, down_t, up, masked, total,
    stage, quad, dt_raw, g, r, x0, sa, sb, sl, sr, xa, xb, xl, xr, y2, y3, u0, u1, u2, u3,
    load_sem, quad_s, quad_r, ag_s, ag_r, sib_s, sib_r, rs_s, rs_r, up_s, up_r,
):
    outer, inner = lax.axis_index("outer"), lax.axis_index("inner")
    core = outer % 2
    me = {"x": inner // 2, "y": (outer // 2) % 4, "z": (inner % 2) * 2 + outer // 8}
    side = {a: 1 - 2 * (me[a] % 2) for a in "xyz"}

    def device(core=core, **at):
        c = dict(me, **at)
        return ((c["z"] % 2) * 8 + c["y"] * 2 + core, c["x"] * 2 + c["z"] // 2)

    def step(axis, by):
        return (me[axis] + by + 4) % 4

    sibling = device(core=1 - core)

    def send(src, dst, s, r_, to):
        copy = pltpu.make_async_remote_copy(
            src_ref=src, dst_ref=dst, send_sem=s, recv_sem=r_, device_id=to, device_id_type=MESH
        )
        copy.start()
        return copy

    barrier = pltpu.get_barrier_semaphore()
    peers = [device(**{a: step(a, by)}) for a in "xyz" for by in (1, 2, 3)]
    xq = me["x"] + 1 - 2 * (me["x"] % 2)
    zq = step("z", 2)
    peers += [device(core=1 - core, z=step("z", by)) for by in range(4)]
    peers += [device(x=xq, z=zq)]
    for peer in peers:
        pl.semaphore_signal(barrier, inc=1, device_id=peer, device_id_type=MESH)

    loads = []
    quarters = [pl.ds(STEP * c, STEP) for c in range(4)]
    for n, (src, dst) in enumerate((
        (frozen_hbm, frozen), (down_hbm, down_t), (cot_hbm, cot), (up_hbm, up),
        (lengths_hbm, lengths),
    ) + tuple((tokens_hbm.at[:, at], tokens.at[:, at]) for at in quarters)):
        loads.append(pltpu.make_async_copy(src, dst, load_sem.at[n]))
        loads[-1].start()

    kx, kz = me["x"] % 2, me["z"] // 2
    mine = kx * 2 + kz
    quad_copies = []

    def fill_stage():
        loads[0].wait()
        stage[...] = jnp.zeros_like(stage)
        for k in range(4):
            stage[k, 0:OWN, :] = frozen[:, 128 * k : 128 * (k + 1)]
        at_home = (me["z"] % 2, me["y"], core, me["x"], me["z"] // 2)
        loads[1].wait()
        dt_raw[at_home] = jnp.concatenate([down_t[...], jnp.zeros((RANK, 128 - OWN), BF16)], axis=1)

    def exchange():
        pl.semaphore_wait(barrier, len(peers))
        for n, (dx, dz) in enumerate(((1, 0), (0, 1), (1, 1))):
            tx, tz = (kx + dx) % 2, (kz + dz) % 2
            to = device(x=xq if dx else me["x"], z=zq if dz else me["z"])
            quad_copies.append(
                send(stage.at[tx * 2 + tz], quad.at[mine], quad_s.at[n], quad_r.at[n], to)
            )

    def piece():
        need(*quad_copies)
        quad[mine] = stage[mine]
        rows = jnp.concatenate([quad[k, 0:OWN, :].astype(F32) for k in range(4)], axis=0)
        w[kx, kz, me["z"] % 2, me["y"], core, me["x"] // 2] = rows.astype(BF16)

    contract = (((1,), (1,)), ((), ()))

    def at_of(kind, at, r0, n):
        x, y, z, c = at["x"], at["y"], at["z"], at["core"]
        whole = lambda v: isinstance(v, slice)
        zhi, zlo = (ALL, ALL) if whole(z) else (z // 2, z % 2)
        rows = pl.ds(r0, n)
        if kind == "down":
            return dt_raw.at[zlo, y, c, x, zhi, rows, :]
        xhi, xlo = (ALL, ALL) if whole(x) else (x // 2, x % 2)
        return w.at[xlo, zhi, zlo, y, c, xhi, rows, :]

    done = set()

    def need(*copies):
        for copy in copies:
            if id(copy) not in done:
                done.add(id(copy))
                copy.wait_recv()

    class Stream:
        def __init__(self, name, n):
            self.n = n
            self.kind, (self.a, self.b, self.c), self.r0, self.rows = STREAMS[name]
            self.cut = self.rows // 32 * 16
            self.copies = {}
            self.sibs = {}

        def ref(self, at, part=None):
            r0, rows = self.r0, self.rows
            if part == 0:
                rows = self.cut
            elif part == 1:
                r0, rows = r0 + self.cut, rows - self.cut
            return at_of(self.kind, {**me, "core": core, **at}, r0, rows)

        def go(self, key, axis, by, at, part=None):
            ref = self.ref(at, part)
            n = len(self.copies)
            self.copies[key] = send(
                ref, ref, ag_s.at[self.n, n], ag_r.at[self.n, n], device(**{axis: step(axis, by)})
            )

        def sib(self, key, at):
            ref = self.ref(at)
            n = len(self.sibs)
            self.sibs[key] = send(ref, ref, sib_s.at[self.n, n], sib_r.at[self.n, n], sibling)

        def open(self, name, axis, at):
            at = {**at, axis: me[axis]}
            self.go(name + "P", axis, side[axis], at)
            self.go(name + "O", axis, -side[axis], at)

        def onward(self, name, end, axis, at):
            d = side[axis] if end == "P" else -side[axis]
            need(self.copies[name + end])
            key = name + ("o" if end == "P" else "p")
            self.go(key, axis, -d, {**at, axis: step(axis, d)}, 0 if end == "P" else 1)

        def close(self, name):
            need(self.copies[name + "o"], self.copies[name + "p"])

        def sub(self, j):
            d = side[self.b]
            return {self.a: ALL, self.b: step(self.b, (0, d, -d, 2)[j])}

        def open1(self):
            for by in (1, 2, 3):
                self.go(f"1{by}", self.a, by, {})

        def close1(self):
            need(*(self.copies[f"1{by}"] for by in (1, 2, 3)))
            self.open("2", self.b, {self.a: ALL})
            self.sib("20", self.sub(0))

        def fwd2(self, end):
            self.onward("2", end, self.b, {self.a: ALL})
            j = 1 if end == "P" else 2
            self.sib(f"2{j}", self.sub(j))

        def close2(self):
            self.close("2")
            self.sib("23", self.sub(3))

        def open3(self, j):
            self.open(f"3{j}", self.c, self.sub(int(j)))

        def fwd3(self, end, j):
            at = self.sub(int(j))
            self.onward(f"3{j}", end, self.c, at)
            d = side[self.c] if end == "P" else -side[self.c]
            self.sib(f"3{j}{end}", {**at, self.c: step(self.c, d)})

        def close3(self, j):
            self.close(f"3{j}")
            self.sib(f"3{j}o", {**self.sub(int(j)), self.c: step(self.c, 2)})

        def need_sib(self, *keys):
            need(*(self.sibs[key] for key in keys))

        def end(self):
            need(*self.copies.values(), *self.sibs.values())
            for copy in list(self.copies.values()) + list(self.sibs.values()):
                copy.wait_send()

    streams = {name: Stream(name, n) for n, name in enumerate(STREAMS)}

    x0_copies = []
    state = {}

    def raised():
        loads[2].wait()
        loads[3].wait()
        loads[4].wait()
        first = (outer % 2 * 8 + inner) * ROWS
        position = first + lax.broadcasted_iota(jnp.int32, (ROWS, KV), 0)
        live = jnp.where(position < lengths[outer // 2], 1.0, 0.0).astype(BF16)
        masked[...] = cot[...] * live
        back = lax.dot_general(masked[...], up[...], contract, preferred_element_type=F32)
        state["raised2"] = back.astype(BF16) * jnp.asarray(adapter_scale, BF16)
        state["raised2_t"] = state["raised2"].astype(F32).T.astype(BF16)
        total[...] = jnp.zeros_like(total)

    def owners(c):
        loads[5 + c].wait()
        for n in range(0, STEP, 256):
            m = min(256, STEP - n)
            g[:, n : n + m] = jnp.dot(
                state["raised2_t"], tokens[:, STEP * c + n : STEP * c + n + m], preferred_element_type=F32
            )
        for i in range(32):
            o, x, zhi = i // 8, i // 2 % 4, i % 2
            piece = g[:, OWN * i : OWN * (i + 1)]
            r[c // 2, 2 * (c % 2) + o // 2, o % 2, x, zhi, :, 0:OWN] = piece
            r[c // 2, 2 * (c % 2) + o // 2, o % 2, x, zhi, :, OWN:128] = jnp.zeros((RANK, 128 - OWN), F32)

    def owners_pair(c):
        zlo, y = c // 2, pl.ds(2 * (c % 2), 2)
        x0_copies.append(
            send(r.at[zlo, y, 1 - core], x0.at[zlo, y], rs_s.at[0, c], rs_r.at[0, c], sibling)
        )

    def add_sibling(c):
        need(x0_copies[c])
        for y in range(2 * (c % 2), 2 * (c % 2) + 2):
            for x in range(4):
                r[c // 2, y, core, x] = r[c // 2, y, core, x] + x0[c // 2, y, x]

    def r_at(at, r0, n):
        z = at["z"]
        zhi, zlo = (ALL, ALL) if isinstance(z, slice) else (z // 2, z % 2)
        return r.at[zlo, at["y"], core, at["x"], zhi, pl.ds(r0, n), :]

    class Sum:
        def __init__(self, n):
            self.n = n
            (self.a, self.b, self.c), self.r0, self.rows, self.cut = SUMS[n]
            self.free = {self.a: ALL, self.b: ALL, self.c: ALL}
            self.sends = []

        def go(self, src, dst, k, axis, by):
            copy = send(src, dst, rs_s.at[1 + self.n, k], rs_r.at[1 + self.n, k], device(**{axis: step(axis, by)}))
            self.sends.append(copy)
            return copy

        def at(self, by, half=None):
            r0, rows = self.r0, self.rows
            if half == 0:
                rows = self.cut
            elif half == 1:
                r0, rows = r0 + self.cut, rows - self.cut
            return r_at({**self.free, self.a: step(self.a, by)}, r0, rows)

        def pack(self, buffer, ref):
            buffer[...] = ref[...].reshape(buffer.shape).astype(BF16)
            return buffer

        def take(self, ref, buffer):
            ref[...] = ref[...] + buffer[...].astype(F32).reshape(ref.shape)

        def first(self):
            n = self.n
            self.ca = self.go(self.pack(sa[n], self.at(2, 0)), xa[n], 0, self.a, 1)
            self.cb = self.go(self.pack(sb[n], self.at(2, 1)), xb[n], 1, self.a, -1)

        def second(self):
            n = self.n
            need(self.ca)
            self.take(self.at(1, 0), xa[n])
            self.cl = self.go(self.pack(sl[n], self.at(1)), xl[n], 2, self.a, 1)
            need(self.cb)
            self.take(self.at(-1, 1), xb[n])
            self.cr = self.go(self.pack(sr[n], self.at(-1)), xr[n], 3, self.a, -1)

        def third(self):
            need(self.cl, self.cr)
            self.take(self.at(0), xl[self.n])
            self.take(self.at(0), xr[self.n])
            self.k = []
            for j, by in enumerate((1, -1, 2)):
                src = r_at({**self.free, self.a: me[self.a], self.b: step(self.b, by)}, self.r0, self.rows)
                self.k.append(self.go(src, y2[self.n].at[j], 4 + j, self.b, by))

        def fourth(self):
            need(*self.k)
            ref = r_at({**me, self.c: ALL}, self.r0, self.rows)
            ref[...] = ref[...] + y2[self.n][0] + y2[self.n][1] + y2[self.n][2]
            self.k = []
            for j, by in enumerate((1, -1, 2)):
                src = r_at({**me, self.c: step(self.c, by)}, self.r0, self.rows)
                self.k.append(self.go(src, y3[self.n].at[j], 7 + j, self.c, by))

        def fifth(self):
            need(*self.k)
            own = r_at(me, self.r0, self.rows)
            total = own[...] + y3[self.n][0] + y3[self.n][1] + y3[self.n][2]
            dgrad[self.r0 : self.r0 + self.rows, :] = total[:, 0:OWN]

        def end(self):
            for copy in self.sends:
                copy.wait_send()

    sums = [Sum(n) for n in range(3)]

    up_copies = []

    def up_send(src, dst, to):
        k = len(up_copies)
        copy = send(src, dst, up_s.at[k], up_r.at[k], to)
        up_copies.append(copy)
        return copy

    others = [(c, by) for c in range(2) for by in range(4) if (c, by) != (0, 0)]

    def up_rows(c, z):
        return pl.ds(pl.multiple_of(c * 32 + z * 8, 8), 8)

    def low_rows():
        down = streams["D"]
        down.need_sib(*down.sibs)
        for c in range(4):
            for i in range(32):
                o, x, zhi = i // 8, i // 2 % 4, i % 2
                piece = dt_raw[c // 2, 2 * (c % 2) + o // 2, o % 2, x, zhi]
                dt[:, OWN * i + STEP * c : OWN * (i + 1) + STEP * c] = piece[:, 0:OWN]

    def low():
        low = jnp.zeros((ROWS, RANK), F32)
        for c in range(29):
            low += lax.dot_general(
                tokens[:, 512 * c : 512 * (c + 1)], dt[:, 512 * c : 512 * (c + 1)], contract,
                preferred_element_type=F32,
            )
        lowered2 = low.astype(BF16) * jnp.asarray(adapter_scale, BF16)
        lowered2_t = lowered2.astype(F32).T.astype(BF16)
        u0[...] = jnp.dot(lowered2_t, masked[...], preferred_element_type=F32)
        state["k"] = []
        for j, (c, by) in enumerate(others):
            to_core, z = core + c - 2 * c * core, step("z", by)
            state["k"].append(up_send(u0.at[up_rows(to_core, z)], u1.at[j], device(core=to_core, z=z)))
        total[...] += jnp.dot(lowered2, up[...], preferred_element_type=F32)

    def wait_up():
        need(*state["k"])

    def up_x():
        wait_up()
        part = u0[up_rows(core, me["z"]), :]
        for j in range(len(others)):
            part = part + u1[j]
        u2[me["x"]] = part
        ref = u2.at[me["x"]]
        state["k"] = [up_send(ref, ref, device(x=step("x", by))) for by in (1, 2, 3)]

    def up_y():
        wait_up()
        u3[me["y"]] = u2[0] + u2[1] + u2[2] + u2[3]
        ref = u3.at[me["y"]]
        state["k"] = [up_send(ref, ref, device(y=step("y", by))) for by in (1, 2, 3)]

    def up_gather():
        wait_up()
        own = up_rows(core, me["z"])
        ugrad[own, :] = u3[0] + u3[1] + u3[2] + u3[3]
        ref = ugrad.at[own]
        state["k"] = [
            up_send(ref, ref, device(core=core + c - 2 * c * core, z=step("z", by))) for c, by in others
        ]

    w3 = w.reshape(4, D, 128)

    def rows_of(j, zlo):
        d = side["y"]
        y = step("y", (0, d, -d, 2)[j])
        odd, early = y % 2, j % 2 == 0
        start = odd * 1920 if early else odd * 1792
        zlo = (me["z"] + 1 + zlo) % 2
        return zlo * 7424 + (y // 2) * STEP + start, 1792 if early else 1920

    def weights(base, size):
        at = pl.ds(pl.multiple_of(base, 128), size)
        return at, jnp.concatenate([w3[k, at, :] for k in range(4)], axis=1)

    def keys_part(j, zlo):
        streams["X"].need_sib(f"2{j}", *(f"3{j}{end}" for end in "POo"))
        streams["Z"].need_sib(*((f"2{j}", f"3{j}o") if zlo else (f"3{j}P", f"3{j}O")))
        if j == 0:
            streams["Y"].need_sib(*(f"2{i}" for i in range(4)))
        else:
            streams["Y"].need_sib(*(f"3{i}{' POo'[j]}" for i in range(4)))
        at, wc = weights(*rows_of(j, zlo))
        total[...] += jnp.dot(tokens[:, at], wc, preferred_element_type=F32)

    def input_part(j, zlo):
        base, size = rows_of(j, zlo)
        for n in range(0, size, 256):
            at, wc = weights(base + n, min(256, size - n))
            out = lax.dot_general(masked[...], wc, contract, preferred_element_type=F32)
            out += jnp.dot(state["raised2"], dt[:, at], preferred_element_type=F32)
            ig[:, at] = out.astype(BF16)

    def add_siblings():
        for c in range(4):
            add_sibling(c)

    D_, Z_, X_, Y_ = streams.values()
    fill_stage()
    raised()
    owners(0)
    exchange()
    D_.open1()
    piece()
    Z_.open1()
    X_.open1()
    Y_.open1()
    owners(1)
    owners(2)
    owners_pair(0)
    owners_pair(1)
    owners_pair(2)
    owners(3)
    owners_pair(3)
    D_.close1()
    D_.open3(0)
    X_.close1()
    X_.open3(0)
    Z_.close1()
    Z_.open3(0)
    add_siblings()
    sums[0].first()
    D_.fwd2("P")
    D_.fwd2("O")
    D_.fwd3("O", 0)
    D_.open3(1)
    D_.open3(2)
    Y_.close1()
    D_.fwd3("P", 0)
    Y_.open3(0)
    X_.fwd2("P")
    X_.open3(1)
    X_.fwd2("O")
    X_.fwd3("O", 0)
    X_.fwd3("P", 0)
    sums[2].first()
    Z_.fwd3("P", 0)
    Z_.fwd3("O", 0)
    D_.close2()
    D_.fwd3("O", 1)
    D_.fwd3("P", 1)
    D_.open3(3)
    sums[1].first()
    Z_.fwd2("P")
    Z_.open3(1)
    D_.fwd3("O", 2)
    D_.fwd3("P", 2)
    Z_.fwd2("O")
    D_.close3(0)
    Y_.fwd2("P")
    Y_.fwd2("O")
    X_.open3(2)
    Y_.open3(1)
    X_.fwd3("P", 1)
    Y_.fwd3("P", 0)
    Y_.fwd3("O", 0)
    X_.fwd3("O", 1)
    X_.close2()
    Z_.close3(0)
    X_.close3(0)
    Z_.open3(2)
    D_.close3(1)
    D_.fwd3("P", 3)
    D_.fwd3("O", 3)
    X_.open3(3)
    Y_.open3(2)
    D_.close3(2)
    Z_.close2()
    Z_.fwd3("P", 1)
    Z_.fwd3("O", 1)
    X_.fwd3("P", 2)
    Y_.close2()
    Y_.fwd3("O", 1)
    X_.fwd3("O", 2)
    Y_.fwd3("P", 1)
    Z_.open3(3)
    sums[0].second()
    keys_part(0, 0)
    Y_.open3(3)
    D_.close3(3)
    keys_part(0, 1)
    X_.close3(1)
    Y_.close3(0)
    low_rows()
    low()
    sums[1].second()
    sums[2].second()
    Z_.fwd3("P", 2)
    Z_.fwd3("O", 2)
    X_.fwd3("P", 3)
    Y_.fwd3("O", 2)
    X_.fwd3("O", 3)
    sums[0].third()
    Y_.fwd3("P", 2)
    Z_.close3(1)
    X_.close3(2)
    Y_.close3(1)
    input_part(0, 0)
    Y_.fwd3("O", 3)
    Y_.fwd3("P", 3)
    Z_.fwd3("P", 3)
    Z_.fwd3("O", 3)
    input_part(0, 1)
    up_x()
    keys_part(2, 0)
    keys_part(1, 0)
    keys_part(1, 1)
    sums[1].third()
    sums[2].third()
    X_.close3(3)
    input_part(1, 0)
    up_y()
    Z_.close3(2)
    input_part(1, 1)
    sums[0].fourth()
    Y_.close3(2)
    Z_.close3(3)
    keys_part(2, 1)
    Y_.close3(3)
    input_part(2, 0)
    input_part(2, 1)
    up_gather()
    sums[2].fourth()
    sums[1].fourth()
    keys_part(3, 0)
    sums[0].fifth()
    keys_part(3, 1)
    input_part(3, 0)
    input_part(3, 1)
    sums[2].fifth()
    wait_up()
    sums[1].fifth()
    keys[...] = total[...].astype(BF16)
    for s in streams.values():
        s.end()
    for s in sums:
        s.end()
    for copy in quad_copies + x0_copies + up_copies:
        copy.wait_send()


PARTS = 8


def store_kernel(ig, keys, dgrad, ugrad, ig_hbm, keys_hbm, dgrad_hbm, ugrad_hbm, sem):
    rows = [pl.ds(n * (ROWS // PARTS), ROWS // PARTS) for n in range(PARTS)]
    pairs = [(ig.at[at], ig_hbm.at[at]) for at in rows]
    pairs += [(keys, keys_hbm), (dgrad, dgrad_hbm), (ugrad, ugrad_hbm)]
    copies = [pltpu.make_async_copy(a, b, sem.at[n]) for n, (a, b) in enumerate(pairs)]
    for copy in copies:
        copy.start()
    for copy in copies:
        copy.wait()


def on_device(tokens, cotangent, lengths, frozen, down_weight, up_weight):
    vmem = pl.BlockSpec(memory_space=pltpu.VMEM)
    anywhere = pl.BlockSpec(memory_space=pl.ANY)
    in_hbm = lambda array: pltpu.with_memory_space_constraint(array, pltpu.HBM)
    down_t = down_weight.T
    def halves(rows):
        return [pltpu.VMEM((16 * rows(n), 128), BF16) for n in range(3)]

    def buffers(shape):
        return [pltpu.VMEM(shape(n), F32) for n in range(3)]

    def cdims(axis):
        return (2, 2) if axis == "z" else (4,)

    scratch = [
        pltpu.VMEM((2, 2, 2, 4, 2, 2, QUAD, 128), BF16),
        pltpu.VMEM((RANK, D), BF16),
        pltpu.VMEM((ROWS, D), BF16),
        pltpu.SMEM((8,), jnp.int32),
        pltpu.VMEM((ROWS, KV), BF16),
        pltpu.VMEM((OWN, KV), BF16),
        pltpu.VMEM((RANK, OWN), BF16),
        pltpu.VMEM((RANK, KV), BF16),
        pltpu.VMEM((ROWS, KV), BF16),
        pltpu.VMEM((ROWS, KV), F32),
        pltpu.VMEM((4, 128, 128), BF16),
        pltpu.VMEM((4, 128, 128), BF16),
        pltpu.VMEM((2, 4, 2, 4, 2, RANK, 128), BF16),
        pltpu.VMEM((RANK, STEP), F32),
        pltpu.VMEM((2, 4, 2, 4, 2, RANK, 128), F32),
        pltpu.VMEM((2, 4, 4, 2, RANK, 128), F32),
        *[halves(lambda n: SUMS[n][3]), halves(lambda n: SUMS[n][2] - SUMS[n][3])],
        *[halves(lambda n: SUMS[n][2]) for _ in range(2)],
        *[halves(lambda n: SUMS[n][3]), halves(lambda n: SUMS[n][2] - SUMS[n][3])],
        *[halves(lambda n: SUMS[n][2]) for _ in range(2)],
        buffers(lambda n: (3,) + cdims(SUMS[n][0][2]) + (SUMS[n][2], 128)),
        buffers(lambda n: (3, SUMS[n][2], 128)),
        pltpu.VMEM((RANK, KV), F32),
        pltpu.VMEM((7, 8, KV), F32),
        pltpu.VMEM((4, 8, KV), F32),
        pltpu.VMEM((4, 8, KV), F32),
        pltpu.SemaphoreType.DMA((9,)),
        pltpu.SemaphoreType.DMA((3,)),
        pltpu.SemaphoreType.DMA((3,)),
        pltpu.SemaphoreType.DMA((4, 24)),
        pltpu.SemaphoreType.DMA((4, 24)),
        pltpu.SemaphoreType.DMA((4, 16)),
        pltpu.SemaphoreType.DMA((4, 16)),
        pltpu.SemaphoreType.DMA((4, 10)),
        pltpu.SemaphoreType.DMA((4, 10)),
        pltpu.SemaphoreType.DMA((20,)),
        pltpu.SemaphoreType.DMA((20,)),
    ]
    shapes = (((ROWS, D), BF16), ((ROWS, KV), BF16), ((RANK, OWN), F32), ((RANK, KV), F32))
    inputs = (lengths, tokens, cotangent, frozen, down_t, up_weight)
    results = pl.pallas_call(
        comm_kernel,
        out_shape=tuple(pltpu.VMEM(*shape) for shape in shapes),
        in_specs=[anywhere] * 6,
        out_specs=(vmem,) * 4,
        scratch_shapes=scratch,
        compiler_params=pltpu.CompilerParams(
            collective_id=0, has_side_effects=True, vmem_limit_bytes=46 * 1024 * 1024
        ),
        name="gather_multiply_sum",
    )(*[in_hbm(array) for array in inputs])
    results = [pltpu.with_memory_space_constraint(array, pltpu.VMEM) for array in results]
    ig, keys, dgrad, ugrad = pl.pallas_call(
        store_kernel,
        out_shape=tuple(jax.ShapeDtypeStruct(*shape) for shape in shapes),
        in_specs=[vmem] * 4,
        out_specs=(anywhere,) * 4,
        scratch_shapes=[pltpu.SemaphoreType.DMA((PARTS + 3,))],
        compiler_params=pltpu.CompilerParams(vmem_limit_bytes=4 * 1024 * 1024),
        name="store",
    )(*results)
    return keys, ig, dgrad.T, ugrad


def solution(mesh):
    return jax.shard_map(
        on_device,
        mesh=mesh,
        in_specs=(
            P(("outer", "inner"), None),
            P(("outer", "inner"), None),
            P(),
            P(("outer", "inner"), None),
            P(("outer", "inner"), None),
            P(),
        ),
        out_specs=(
            P(("outer", "inner"), None),
            P(("outer", "inner"), None),
            P(("outer", "inner"), None),
            P(),
        ),
        check_vma=False,
    )
```

```python
import jax
import jax.numpy as jnp
from jax import lax
from jax.experimental import pallas as pl
from jax.experimental.pallas import tpu as pltpu
from jax.sharding import PartitionSpec as P

MESH = pl.DeviceIdType.MESH
F32, BF16 = jnp.float32, jnp.bfloat16

D, KV, RANK, SEQ_LEN, ROWS, OWN = 14848, 512, 64, 4096, 256, 116
QUAD = 4 * OWN
STEP = 3712
adapter_scale = 2.0
BEHIND = 90

STREAMS = {
    "D": ("down", "yxz", 0, 64),
    "Z": ("w", "xyz", 0, 160),
    "X": ("w", "zyx", 160, 176),
    "Y": ("w", "zxy", 336, 128),
}
SUMS = (("xyz", 0, 24, 8), ("yzx", 24, 24, 16), ("zxy", 48, 16, 8))
ALL = slice(None)


CONTRACT = (((1,), (1,)), ((), ()))


def place(outer, inner):
    return {"x": inner // 2, "y": (outer // 2) % 4, "z": (inner % 2) * 2 + outer // 8}


def rows_of(me, j, own):
    d = 1 - 2 * (me["y"] % 2)
    y = (me["y"] + (0, d, -d, 2)[j] + 4) % 4
    odd, early = y % 2, j % 2 == 0
    start = odd * 1920 if early else odd * 1792
    zlo = (me["z"] + 1 + own) % 2
    return zlo * 7424 + (y // 2) * STEP + start, 1792 if early else 1920


def weights(w3, base, size):
    at = pl.ds(pl.multiple_of(base, 128), size)
    return at, jnp.concatenate([w3[k, at, :] for k in range(4)], axis=1)


def input_columns(w3, dt, masked, raised2, base, size):
    at, wc = weights(w3, base, size)
    out = lax.dot_general(masked[...], wc, CONTRACT, preferred_element_type=F32)
    out += jnp.dot(raised2, dt[:, at], preferred_element_type=F32)
    return out.astype(BF16)


def comm_kernel(
    lengths_hbm, tokens_hbm, cot_hbm, frozen_hbm, down_hbm, up_hbm,
    ig, total, dgrad, ugrad, w_last, dt_last, tokens_last, masked, raised_out,
    w, dt, tokens, lengths, cot, frozen, down_t, up,
    stage, quad, dt_raw, g, r, x0, sa, sb, sl, sr, sy, xa, xb, xl, xr, y2, y3, u0, u1, u2, u3,
    load_sem, quad_s, quad_r, ag_s, ag_r, sib_s, sib_r, rs_s, rs_r, up_s, up_r,
):
    outer, inner = lax.axis_index("outer"), lax.axis_index("inner")
    core = outer % 2
    me = place(outer, inner)
    side = {a: 1 - 2 * (me[a] % 2) for a in "xyz"}

    def device(core=core, **at):
        c = dict(me, **at)
        return ((c["z"] % 2) * 8 + c["y"] * 2 + core, c["x"] * 2 + c["z"] // 2)

    def step(axis, by):
        return (me[axis] + by + 4) % 4

    sibling = device(core=1 - core)

    def send(src, dst, s, r_, to):
        copy = pltpu.make_async_remote_copy(
            src_ref=src, dst_ref=dst, send_sem=s, recv_sem=r_, device_id=to, device_id_type=MESH
        )
        copy.start()
        sent.append(copy)
        if len(sent) > BEHIND:
            left(sent[len(sent) - 1 - BEHIND])
        return copy

    gone = set()

    def left(copy):
        if id(copy) not in gone:
            gone.add(id(copy))
            copy.wait_send()

    sent = []

    barrier = pltpu.get_barrier_semaphore()
    peers = [device(**{a: step(a, by)}) for a in "xyz" for by in (1, 2, 3)]
    xq = me["x"] + 1 - 2 * (me["x"] % 2)
    zq = step("z", 2)
    peers += [device(core=1 - core, z=step("z", by)) for by in range(4)]
    peers += [device(x=xq, z=zq)]
    for peer in peers:
        pl.semaphore_signal(barrier, inc=1, device_id=peer, device_id_type=MESH)

    loads = []
    quarters = [pl.ds(STEP * c, STEP) for c in range(4)]
    for n, (src, dst) in enumerate((
        (frozen_hbm, frozen), (down_hbm, down_t), (cot_hbm, cot), (up_hbm, up),
        (lengths_hbm, lengths),
    ) + tuple((tokens_hbm.at[:, at], tokens.at[:, at]) for at in quarters)):
        loads.append(pltpu.make_async_copy(src, dst, load_sem.at[n]))
        loads[-1].start()

    kx, kz = me["x"] % 2, me["z"] // 2
    mine = kx * 2 + kz
    quad_copies = []

    def fill_stage():
        loads[0].wait()
        stage[...] = jnp.zeros_like(stage)
        for k in range(4):
            stage[k, 0:OWN, :] = frozen[:, 128 * k : 128 * (k + 1)]
        at_home = (me["z"] % 2, me["y"], core, me["x"], me["z"] // 2)
        loads[1].wait()
        dt_raw[at_home] = jnp.concatenate([down_t[...], jnp.zeros((RANK, 128 - OWN), BF16)], axis=1)

    def enter():
        pl.semaphore_wait(barrier, len(peers))

    def exchange():
        for n, (dx, dz) in enumerate(((1, 0), (0, 1), (1, 1))):
            tx, tz = (kx + dx) % 2, (kz + dz) % 2
            to = device(x=xq if dx else me["x"], z=zq if dz else me["z"])
            quad_copies.append(
                send(stage.at[tx * 2 + tz], quad.at[mine], quad_s.at[n], quad_r.at[n], to)
            )

    def piece():
        need(*quad_copies)
        quad[mine] = stage[mine]
        rows = jnp.concatenate([quad[k, 0:OWN, :].astype(F32) for k in range(4)], axis=0)
        w[kx, kz, me["z"] % 2, me["y"], core, me["x"] // 2] = rows.astype(BF16)

    def at_of(kind, at, r0, n):
        x, y, z, c = at["x"], at["y"], at["z"], at["core"]
        whole = lambda v: isinstance(v, slice)
        zhi, zlo = (ALL, ALL) if whole(z) else (z // 2, z % 2)
        rows = pl.ds(r0, n)
        if kind == "down":
            return dt_raw.at[zlo, y, c, x, zhi, rows, :]
        xhi, xlo = (ALL, ALL) if whole(x) else (x // 2, x % 2)
        return w.at[xlo, zhi, zlo, y, c, xhi, rows, :]

    done = set()

    def need(*copies):
        for copy in copies:
            if id(copy) not in done:
                done.add(id(copy))
                copy.wait_recv()

    class Stream:
        def __init__(self, name, n):
            self.n = n
            self.kind, (self.a, self.b, self.c), self.r0, self.rows = STREAMS[name]
            self.cut = self.rows // 32 * 16
            self.direct = name == "D"
            self.copies = {}
            self.sibs = {}

        def ref(self, at, part=None):
            r0, rows = self.r0, self.rows
            if part == 0:
                rows = self.cut
            elif part == 1:
                r0, rows = r0 + self.cut, rows - self.cut
            return at_of(self.kind, {**me, "core": core, **at}, r0, rows)

        def go(self, key, axis, by, at, part=None):
            ref = self.ref(at, part)
            n = len(self.copies)
            self.copies[key] = send(
                ref, ref, ag_s.at[self.n, n], ag_r.at[self.n, n], device(**{axis: step(axis, by)})
            )

        def sib(self, key, at):
            ref = self.ref(at)
            n = len(self.sibs)
            self.sibs[key] = send(ref, ref, sib_s.at[self.n, n], sib_r.at[self.n, n], sibling)

        def both(self, name, axis, at, k=""):
            at = {**at, axis: me[axis]}
            for end, by in (("P", side[axis]), ("O", -side[axis])):
                self.go(name + end + k, axis, by, at)

        def need_all(self, start):
            need(*(copy for key, copy in self.copies.items() if key[: len(start)] == start))

        def onward(self, name, end, axis, at):
            d = side[axis] if end == "P" else -side[axis]
            self.need_all(name + end)
            if self.direct and name == "2":
                return
            key = name + ("o" if end == "P" else "p")
            self.go(key, axis, -d, {**at, axis: step(axis, d)}, 0 if end == "P" else 1)

        def close(self, name):
            need(self.copies[name + "o"], self.copies[name + "p"])

        def sub(self, j):
            d = side[self.b]
            return {self.a: ALL, self.b: step(self.b, (0, d, -d, 2)[j])}

        def open1(self):
            for k in (1, 2, 3):
                self.go(f"1{k}", self.a, k, {})

        def row(self, k):
            if k:
                need(self.copies[f"1{k}"])
            return {self.a: step(self.a, -k)}

        def open2(self, k):
            self.both("2", self.b, self.row(k), str(k))
            if self.direct:
                self.go(f"2X{k}", self.b, 2, self.row(k))

        def open30(self, k):
            self.both("30", self.c, self.row(k), str(k))

        def close1(self):
            self.sib("20", self.sub(0))

        def fwd2(self, end):
            self.onward("2", end, self.b, {self.a: ALL})
            j = 1 if end == "P" else 2
            self.sib(f"2{j}", self.sub(j))

        def close2(self):
            if self.direct:
                self.need_all("2X")
            else:
                self.close("2")
            self.sib("23", self.sub(3))

        def open3(self, j):
            self.both(f"3{j}", self.c, self.sub(j))

        def fwd3(self, end, j):
            at = self.sub(j)
            self.onward(f"3{j}", end, self.c, at)
            d = side[self.c] if end == "P" else -side[self.c]
            self.sib(f"3{j}{end}", {**at, self.c: step(self.c, d)})

        def close3(self, j):
            self.close(f"3{j}")
            self.sib(f"3{j}o", {**self.sub(j), self.c: step(self.c, 2)})

        def need_sib(self, *keys):
            need(*(self.sibs[key] for key in keys))

    streams = {name: Stream(name, n) for n, name in enumerate(STREAMS)}

    x0_copies = {}
    state = {}

    def raised():
        loads[2].wait()
        loads[3].wait()
        loads[4].wait()
        first = (outer % 2 * 8 + inner) * ROWS
        position = first + lax.broadcasted_iota(jnp.int32, (ROWS, KV), 0)
        live = jnp.where(position < lengths[outer // 2], 1.0, 0.0).astype(BF16)
        masked[...] = cot[...] * live
        back = lax.dot_general(masked[...], up[...], CONTRACT, preferred_element_type=F32)
        state["raised2"] = back.astype(BF16) * jnp.asarray(adapter_scale, BF16)
        raised_out[...] = state["raised2"]
        state["raised2_t"] = state["raised2"].astype(F32).T.astype(BF16)
        total[...] = jnp.zeros_like(total)

    def owners(c):
        loads[5 + c].wait()
        for n in range(0, STEP, 256):
            m = min(256, STEP - n)
            g[:, n : n + m] = jnp.dot(
                state["raised2_t"], tokens[:, STEP * c + n : STEP * c + n + m], preferred_element_type=F32
            )
        for i in range(32):
            o, x, zhi = i // 8, i // 2 % 4, i % 2
            piece = g[:, OWN * i : OWN * (i + 1)]
            r[c // 2, 2 * (c % 2) + o // 2, o % 2, x, zhi, :, 0:OWN] = piece
            r[c // 2, 2 * (c % 2) + o // 2, o % 2, x, zhi, :, OWN:128] = jnp.zeros((RANK, 128 - OWN), F32)

    def owners_pair(c):
        zlo, y = c // 2, pl.ds(2 * (c % 2), 2)
        x0_copies[c] = send(r.at[zlo, y, 1 - core], x0.at[zlo, y], rs_s.at[0, c], rs_r.at[0, c], sibling)

    def add_sibling(c):
        need(x0_copies[c])
        for y in range(2 * (c % 2), 2 * (c % 2) + 2):
            for x in range(4):
                r[c // 2, y, core, x] = r[c // 2, y, core, x] + x0[c // 2, y, x]

    def r_at(at, r0, n):
        z = at["z"]
        zhi, zlo = (ALL, ALL) if isinstance(z, slice) else (z // 2, z % 2)
        return r.at[zlo, at["y"], core, at["x"], zhi, pl.ds(r0, n), :]

    class Sum:
        def __init__(self, n):
            self.n = n
            (self.a, self.b, self.c), self.r0, self.rows, self.cut = SUMS[n]
            self.free = {self.a: ALL, self.b: ALL, self.c: ALL}
            self.sends = []

        def go(self, src, dst, k, axis, by):
            copy = send(src, dst, rs_s.at[1 + self.n, k], rs_r.at[1 + self.n, k], device(**{axis: step(axis, by)}))
            self.sends.append(copy)
            return copy

        def at(self, by, half=None):
            r0, rows = self.r0, self.rows
            if half == 0:
                rows = self.cut
            elif half == 1:
                r0, rows = r0 + self.cut, rows - self.cut
            return r_at({**self.free, self.a: step(self.a, by)}, r0, rows)

        def pack(self, buffer, ref):
            buffer[...] = ref[...].reshape(buffer.shape).astype(BF16)
            return buffer

        def take(self, ref, buffer):
            ref[...] = ref[...] + buffer[...].astype(F32).reshape(ref.shape)

        def first(self):
            n = self.n
            self.ca = self.go(self.pack(sa[n], self.at(2, 0)), xa[n], 0, self.a, 1)
            self.cb = self.go(self.pack(sb[n], self.at(2, 1)), xb[n], 1, self.a, -1)

        def second(self):
            n = self.n
            need(self.ca)
            self.take(self.at(1, 0), xa[n])
            self.cl = self.go(self.pack(sl[n], self.at(1)), xl[n], 2, self.a, 1)
            need(self.cb)
            self.take(self.at(-1, 1), xb[n])
            self.cr = self.go(self.pack(sr[n], self.at(-1)), xr[n], 3, self.a, -1)

        def third(self):
            need(self.cl, self.cr)
            self.take(self.at(0), xl[self.n])
            self.take(self.at(0), xr[self.n])
            self.k = []
            for j, by in enumerate((1, -1, 2)):
                src = r_at({**self.free, self.a: me[self.a], self.b: step(self.b, by)}, self.r0, self.rows)
                out = self.pack(sy[self.n].at[j], src)
                self.k.append(self.go(out, y2[self.n].at[j], 4 + j, self.b, by))

        def fourth(self):
            need(*self.k)
            ref = r_at({**me, self.c: ALL}, self.r0, self.rows)
            for j in range(3):
                self.take(ref, y2[self.n].at[j])
            self.k = []
            for j, by in enumerate((1, -1, 2)):
                src = r_at({**me, self.c: step(self.c, by)}, self.r0, self.rows)
                self.k.append(self.go(src, y3[self.n].at[j], 7 + j, self.c, by))

        def fifth(self):
            need(*self.k)
            own = r_at(me, self.r0, self.rows)
            total = own[...] + y3[self.n][0] + y3[self.n][1] + y3[self.n][2]
            dgrad[self.r0 : self.r0 + self.rows, :] = total[:, 0:OWN]

    sums = [Sum(n) for n in range(3)]

    up_copies = []

    def up_send(src, dst, to):
        k = len(up_copies)
        copy = send(src, dst, up_s.at[k], up_r.at[k], to)
        up_copies.append(copy)
        return copy

    others = [(c, by) for c in range(2) for by in range(4) if (c, by) != (0, 0)]

    def up_rows(c, z):
        return pl.ds(pl.multiple_of(c * 32 + z * 8, 8), 8)

    def low_rows():
        down = streams["D"]
        down.need_sib(*down.sibs)
        for c in range(4):
            for i in range(32):
                o, x, zhi = i // 8, i // 2 % 4, i % 2
                piece = dt_raw[c // 2, 2 * (c % 2) + o // 2, o % 2, x, zhi]
                dt[:, OWN * i + STEP * c : OWN * (i + 1) + STEP * c] = piece[:, 0:OWN]

    def low():
        base, size = rows_of(me, 3, 1)
        at = pl.ds(pl.multiple_of(base, 128), size)
        dt_last[...] = dt[:, at]
        tokens_last[...] = tokens[:, at]
        low = jnp.zeros((ROWS, RANK), F32)
        for c in range(29):
            low += lax.dot_general(
                tokens[:, 512 * c : 512 * (c + 1)], dt[:, 512 * c : 512 * (c + 1)], CONTRACT,
                preferred_element_type=F32,
            )
        lowered2 = low.astype(BF16) * jnp.asarray(adapter_scale, BF16)
        lowered2_t = lowered2.astype(F32).T.astype(BF16)
        u0[...] = jnp.dot(lowered2_t, masked[...], preferred_element_type=F32)
        state["k"] = []
        for j, (c, by) in enumerate(others):
            to_core, z = core + c - 2 * c * core, step("z", by)
            state["k"].append(up_send(u0.at[up_rows(to_core, z)], u1.at[j], device(core=to_core, z=z)))
        total[...] += jnp.dot(lowered2, up[...], preferred_element_type=F32)

    def wait_up():
        need(*state["k"])

    def up_x():
        wait_up()
        part = u0[up_rows(core, me["z"]), :]
        for j in range(len(others)):
            part = part + u1[j]
        u2[me["x"]] = part
        ref = u2.at[me["x"]]
        state["k"] = [up_send(ref, ref, device(x=step("x", by))) for by in (1, 2, 3)]

    def up_y():
        wait_up()
        u3[me["y"]] = u2[0] + u2[1] + u2[2] + u2[3]
        ref = u3.at[me["y"]]
        state["k"] = [up_send(ref, ref, device(y=step("y", by))) for by in (1, 2, 3)]

    def up_gather():
        wait_up()
        own = up_rows(core, me["z"])
        ugrad[own, :] = u3[0] + u3[1] + u3[2] + u3[3]
        ref = ugrad.at[own]
        state["k"] = [
            up_send(ref, ref, device(core=core + c - 2 * c * core, z=step("z", by))) for c, by in others
        ]

    w3 = w.reshape(4, D, 128)

    def arrived(j, zlo):
        streams["X"].need_sib(f"2{j}", *(f"3{j}{end}" for end in "POo"))
        streams["Z"].need_sib(*((f"2{j}", f"3{j}o") if zlo else (f"3{j}P", f"3{j}O")))
        subs = ((0, 3) if zlo else (1, 2)) if streams["Y"].b == "z" else range(4)
        streams["Y"].need_sib(*(f"3{i}{' POo'[j]}" if j else f"2{i}" for i in subs))

    def keys_part(j, zlo):
        arrived(j, zlo)
        at, wc = weights(w3, *rows_of(me, j, zlo))
        total[...] += jnp.dot(tokens[:, at], wc, preferred_element_type=F32)

    def last_rows():
        arrived(3, 1)
        at, _ = weights(w3, *rows_of(me, 3, 1))
        w_last[...] = w3[:, at, :]

    def input_part(j, zlo):
        base, size = rows_of(me, j, zlo)
        for n in range(0, size, 256):
            m = min(256, size - n)
            ig[:, pl.ds(pl.multiple_of(base + n, 128), m)] = input_columns(
                w3, dt, masked, state["raised2"], base + n, m
            )

    def add_siblings():
        for c in range(4):
            add_sibling(c)

    D_, Z_, X_, Y_ = streams.values()
    fill_stage()
    raised()
    owners(0)
    enter()
    owners_pair(0)
    D_.open1()
    exchange()
    owners(2)
    owners(3)
    owners_pair(3)
    D_.open2(0)
    owners_pair(2)
    owners(1)
    owners_pair(1)
    D_.open30(2)
    D_.open2(1)
    D_.open30(1)
    D_.open2(2)
    D_.open30(0)
    D_.open30(3)
    D_.open2(3)
    D_.close1()
    piece()
    Z_.open1()
    Z_.open2(0)
    Y_.open1()
    Y_.open2(0)
    Y_.open30(0)
    X_.open1()
    X_.open2(0)
    add_siblings()
    sums[1].first()
    X_.open30(0)
    D_.fwd3("P", 0)
    D_.fwd3("O", 0)
    D_.fwd2("P")
    D_.fwd2("O")
    D_.open3(2)
    D_.open3(1)
    sums[0].first()
    Y_.open2(1)
    Y_.open30(1)
    Y_.open2(2)
    D_.close2()
    D_.open3(3)
    Y_.open30(2)
    Z_.open2(1)
    Z_.open2(2)
    Y_.open2(3)
    Y_.close1()
    X_.open2(1)
    X_.open2(2)
    Z_.open2(3)
    Z_.close1()
    X_.open30(1)
    X_.open2(3)
    X_.close1()
    D_.close3(0)
    X_.open30(3)
    sums[2].first()
    Z_.open30(2)
    D_.fwd3("P", 2)
    D_.fwd3("O", 2)
    X_.open30(2)
    sums[0].second()
    Y_.fwd2("P")
    Z_.open30(1)
    D_.fwd3("O", 1)
    D_.fwd3("P", 1)
    Y_.open30(3)
    Y_.fwd2("O")
    Y_.open3(1)
    D_.fwd3("P", 3)
    D_.fwd3("O", 3)
    sums[2].second()
    X_.fwd3("P", 0)
    Z_.fwd2("O")
    Z_.fwd2("P")
    X_.fwd3("O", 0)
    X_.fwd2("O")
    D_.close3(2)
    Z_.open30(3)
    X_.fwd2("P")
    Y_.fwd3("O", 0)
    Z_.open30(0)
    Y_.fwd3("P", 0)
    X_.open3(1)
    D_.close3(1)
    sums[0].third()
    Z_.open3(1)
    D_.close3(3)
    Y_.close2()
    Y_.fwd3("O", 1)
    low_rows()
    X_.close3(0)
    Y_.fwd3("P", 1)
    X_.open3(2)
    sums[2].third()
    Z_.fwd3("P", 0)
    Z_.fwd3("O", 0)
    low()
    X_.fwd3("P", 1)
    X_.close2()
    Y_.open3(2)
    Z_.open3(2)
    Z_.close2()
    keys_part(0, 0)
    X_.fwd3("O", 1)
    Z_.fwd3("P", 1)
    Z_.fwd3("O", 1)
    input_part(0, 0)
    Y_.open3(3)
    sums[0].fourth()
    Z_.close3(0)
    Y_.close3(0)
    Y_.close3(1)
    X_.open3(3)
    up_x()
    X_.fwd3("P", 2)
    keys_part(0, 1)
    X_.fwd3("O", 2)
    sums[1].second()
    input_part(0, 1)
    Y_.fwd3("O", 2)
    Y_.fwd3("P", 2)
    Z_.open3(3)
    sums[2].fourth()
    Z_.fwd3("O", 2)
    Z_.fwd3("P", 2)
    X_.close3(1)
    Y_.fwd3("O", 3)
    Y_.fwd3("P", 3)
    Z_.close3(1)
    sums[0].fifth()
    keys_part(1, 0)
    sums[1].third()
    X_.fwd3("P", 3)
    X_.fwd3("O", 3)
    input_part(1, 0)
    up_y()
    keys_part(1, 1)
    sums[2].fifth()
    Z_.fwd3("P", 3)
    X_.close3(2)
    Z_.fwd3("O", 3)
    input_part(1, 1)
    Z_.close3(2)
    Y_.close3(2)
    Y_.close3(3)
    keys_part(2, 0)
    input_part(2, 0)
    X_.close3(3)
    sums[1].fourth()
    up_gather()
    keys_part(2, 1)
    input_part(2, 1)
    Z_.close3(3)
    keys_part(3, 0)
    input_part(3, 0)
    last_rows()
    sums[1].fifth()
    wait_up()
    for s in streams.values():
        need(*s.copies.values(), *s.sibs.values())
    for copy in sent:
        left(copy)


def last_kernel(
    ig, total, dgrad, ugrad, w, dt, tokens, masked, raised2,
    keys_hbm, ig_hbm, dgrad_hbm, ugrad_hbm,
    last, keys, sem,
):
    outer, inner = lax.axis_index("outer"), lax.axis_index("inner")
    me = place(outer, inner)
    copies = []

    def store(src, dst):
        copies.append(pltpu.make_async_copy(src, dst, sem.at[len(copies)]))
        copies[-1].start()

    zlo, pair = me["z"] % 2, me["y"] // 2
    early, early_size = rows_of(me, 2, 1)
    for base, size in (
        ((1 - zlo) * 7424, 7424), (zlo * 7424 + pair * STEP, STEP), (early, early_size)
    ):
        at = pl.ds(pl.multiple_of(base, 128), size)
        store(ig.at[:, at], ig_hbm.at[:, at])
    store(dgrad, dgrad_hbm)
    store(ugrad, ugrad_hbm)
    base, size = rows_of(me, 3, 1)
    for n in range(0, size, 640):
        for k in range(n, n + 640, 256):
            m = min(256, n + 640 - k)
            last[:, k : k + m] = input_columns(w, dt, masked, raised2[...], k, m)
        at = pl.ds(pl.multiple_of(base + n, 128), 640)
        store(last.at[:, n : n + 640], ig_hbm.at[:, at])
    _, wc = weights(w, 0, size)
    out = total[...] + jnp.dot(tokens[...], wc, preferred_element_type=F32)
    keys[...] = out.astype(BF16)
    store(keys, keys_hbm)
    for copy in copies:
        copy.wait()


def on_device(tokens, cotangent, lengths, frozen, down_weight, up_weight):
    vmem = pl.BlockSpec(memory_space=pltpu.VMEM)
    anywhere = pl.BlockSpec(memory_space=pl.ANY)
    in_hbm = lambda array: pltpu.with_memory_space_constraint(array, pltpu.HBM)
    down_t = down_weight.T
    def halves(rows):
        return [pltpu.VMEM((16 * rows(n), 128), BF16) for n in range(3)]

    def fours():
        return [pltpu.VMEM((3, 4 * SUMS[n][2], 128), BF16) for n in range(3)]

    def buffers(shape):
        return [pltpu.VMEM(shape(n), F32) for n in range(3)]

    scratch = [
        pltpu.VMEM((2, 2, 2, 4, 2, 2, QUAD, 128), BF16),
        pltpu.VMEM((RANK, D), BF16),
        pltpu.VMEM((ROWS, D), BF16),
        pltpu.SMEM((8,), jnp.int32),
        pltpu.VMEM((ROWS, KV), BF16),
        pltpu.VMEM((OWN, KV), BF16),
        pltpu.VMEM((RANK, OWN), BF16),
        pltpu.VMEM((RANK, KV), BF16),
        pltpu.VMEM((4, 128, 128), BF16),
        pltpu.VMEM((4, 128, 128), BF16),
        pltpu.VMEM((2, 4, 2, 4, 2, RANK, 128), BF16),
        pltpu.VMEM((RANK, STEP), F32),
        pltpu.VMEM((2, 4, 2, 4, 2, RANK, 128), F32),
        pltpu.VMEM((2, 4, 4, 2, RANK, 128), F32),
        *[halves(lambda n: SUMS[n][3]), halves(lambda n: SUMS[n][2] - SUMS[n][3])],
        *[halves(lambda n: SUMS[n][2]) for _ in range(2)],
        fours(),
        *[halves(lambda n: SUMS[n][3]), halves(lambda n: SUMS[n][2] - SUMS[n][3])],
        *[halves(lambda n: SUMS[n][2]) for _ in range(2)],
        fours(),
        buffers(lambda n: (3, SUMS[n][2], 128)),
        pltpu.VMEM((RANK, KV), F32),
        pltpu.VMEM((7, 8, KV), F32),
        pltpu.VMEM((4, 8, KV), F32),
        pltpu.VMEM((4, 8, KV), F32),
        pltpu.SemaphoreType.DMA((9,)),
        pltpu.SemaphoreType.DMA((3,)),
        pltpu.SemaphoreType.DMA((3,)),
        pltpu.SemaphoreType.DMA((4, 40)),
        pltpu.SemaphoreType.DMA((4, 40)),
        pltpu.SemaphoreType.DMA((4, 16)),
        pltpu.SemaphoreType.DMA((4, 16)),
        pltpu.SemaphoreType.DMA((4, 10)),
        pltpu.SemaphoreType.DMA((4, 10)),
        pltpu.SemaphoreType.DMA((20,)),
        pltpu.SemaphoreType.DMA((20,)),
    ]
    grads = [((RANK, OWN), F32), ((RANK, KV), F32)]
    shapes = [((ROWS, D), BF16), ((ROWS, KV), F32)] + grads
    shapes += [((4, 1920, 128), BF16), ((RANK, 1920), BF16), ((ROWS, 1920), BF16)]
    shapes += [((ROWS, KV), BF16), ((ROWS, RANK), BF16)]
    inputs = (lengths, tokens, cotangent, frozen, down_t, up_weight)
    results = pl.pallas_call(
        comm_kernel,
        out_shape=tuple(pltpu.VMEM(*shape) for shape in shapes),
        in_specs=[anywhere] * 6,
        out_specs=(vmem,) * len(shapes),
        scratch_shapes=scratch,
        compiler_params=pltpu.CompilerParams(
            collective_id=0, has_side_effects=True, vmem_limit_bytes=46 * 1024 * 1024
        ),
        name="gather_multiply_sum",
    )(*[in_hbm(array) for array in inputs])
    results = [pltpu.with_memory_space_constraint(array, pltpu.VMEM) for array in results]
    outs = [((ROWS, KV), BF16), ((ROWS, D), BF16)] + grads
    keys, ig, dgrad, ugrad = pl.pallas_call(
        last_kernel,
        out_shape=tuple(jax.ShapeDtypeStruct(*shape) for shape in outs),
        in_specs=[vmem] * len(results),
        out_specs=(anywhere,) * 4,
        scratch_shapes=[
            pltpu.VMEM((ROWS, 1920), BF16),
            pltpu.VMEM((ROWS, KV), BF16),
            pltpu.SemaphoreType.DMA((9,)),
        ],
        compiler_params=pltpu.CompilerParams(vmem_limit_bytes=8 * 1024 * 1024),
        name="last_products",
    )(*results)
    return keys, ig, dgrad.T, ugrad


def solution(mesh):
    return jax.shard_map(
        on_device,
        mesh=mesh,
        in_specs=(
            P(("outer", "inner"), None),
            P(("outer", "inner"), None),
            P(),
            P(("outer", "inner"), None),
            P(("outer", "inner"), None),
            P(),
        ),
        out_specs=(
            P(("outer", "inner"), None),
            P(("outer", "inner"), None),
            P(("outer", "inner"), None),
            P(),
        ),
        check_vma=False,
    )
```

```python
import jax
import jax.numpy as jnp
from jax import lax
from jax.experimental import pallas as pl
from jax.experimental.pallas import tpu as pltpu
from jax.sharding import PartitionSpec as P

MESH = pl.DeviceIdType.MESH
F32, BF16 = jnp.float32, jnp.bfloat16

D, KV, RANK, SEQ_LEN, ROWS, OWN = 14848, 512, 64, 4096, 256, 116
QUAD = 4 * OWN
STEP = 3712
adapter_scale = 2.0
BEHIND = 90

STREAMS = {
    "D": ("down", "yxz", 0, 64),
    "Z": ("w", "xyz", 0, 176),
    "X": ("w", "zyx", 176, 176),
    "Y": ("w", "zxy", 352, 112),
}
SUMS = (("xyz", 0, 24, 8), ("yzx", 24, 24, 16), ("zxy", 48, 16, 8))
ALL = slice(None)


CONTRACT = (((1,), (1,)), ((), ()))


def place(outer, inner):
    return {"x": inner // 2, "y": (outer // 2) % 4, "z": (inner % 2) * 2 + outer // 8}


def rows_of(me, j, own):
    d = 1 - 2 * (me["y"] % 2)
    y = (me["y"] + (0, d, -d, 2)[j] + 4) % 4
    odd, early = y % 2, j % 2 == 0
    start = odd * 1920 if early else odd * 1792
    zlo = (me["z"] + 1 + own) % 2
    return zlo * 7424 + (y // 2) * STEP + start, 1792 if early else 1920


def weights(w3, base, size):
    at = pl.ds(pl.multiple_of(base, 128), size)
    return at, jnp.concatenate([w3[k, at, :] for k in range(4)], axis=1)


def input_columns(w3, dt, masked, raised2, base, size):
    at, wc = weights(w3, base, size)
    out = lax.dot_general(masked[...], wc, CONTRACT, preferred_element_type=F32)
    out += jnp.dot(raised2, dt[:, at], preferred_element_type=F32)
    return out.astype(BF16)


def comm_kernel(
    lengths_hbm, tokens_hbm, cot_hbm, frozen_hbm, down_hbm, up_hbm,
    ig, total, dgrad, ugrad, w_last, dt_last, tokens_last, masked, raised_out,
    w, dt, tokens, lengths, cot, frozen, down_t, up,
    stage, quad, dt_raw, g, r, x0, sa, sb, sl, sr, sy, xa, xb, xl, xr, y2, y3, u0, u1, u2, u3, low_sum,
    load_sem, quad_s, quad_r, ag_s, ag_r, sib_s, sib_r, rs_s, rs_r, up_s, up_r,
):
    outer, inner = lax.axis_index("outer"), lax.axis_index("inner")
    core = outer % 2
    me = place(outer, inner)
    side = {a: 1 - 2 * (me[a] % 2) for a in "xyz"}

    def device(core=core, **at):
        c = dict(me, **at)
        return ((c["z"] % 2) * 8 + c["y"] * 2 + core, c["x"] * 2 + c["z"] // 2)

    def step(axis, by):
        return (me[axis] + by + 4) % 4

    sibling = device(core=1 - core)

    def send(src, dst, s, r_, to):
        copy = pltpu.make_async_remote_copy(
            src_ref=src, dst_ref=dst, send_sem=s, recv_sem=r_, device_id=to, device_id_type=MESH
        )
        copy.start()
        sent.append(copy)
        if len(sent) > BEHIND:
            left(sent[len(sent) - 1 - BEHIND])
        return copy

    gone = set()

    def left(copy):
        if id(copy) not in gone:
            gone.add(id(copy))
            copy.wait_send()

    sent = []

    barrier = pltpu.get_barrier_semaphore()
    peers = [device(**{a: step(a, by)}) for a in "xyz" for by in (1, 2, 3)]
    xq = me["x"] + 1 - 2 * (me["x"] % 2)
    zq = step("z", 2)
    peers += [device(core=1 - core, z=step("z", by)) for by in range(4)]
    peers += [device(x=xq, z=zq)]
    for peer in peers:
        pl.semaphore_signal(barrier, inc=1, device_id=peer, device_id_type=MESH)

    loads = []
    quarters = [pl.ds(STEP * c, STEP) for c in range(4)]
    for n, (src, dst) in enumerate((
        (frozen_hbm, frozen), (down_hbm, down_t), (cot_hbm, cot), (up_hbm, up),
        (lengths_hbm, lengths),
    ) + tuple((tokens_hbm.at[:, at], tokens.at[:, at]) for at in quarters)):
        loads.append(pltpu.make_async_copy(src, dst, load_sem.at[n]))
        loads[-1].start()

    kx, kz = me["x"] % 2, me["z"] // 2
    mine = kx * 2 + kz
    quad_copies = []

    def fill_stage():
        loads[0].wait()
        stage[...] = jnp.zeros_like(stage)
        for k in range(4):
            stage[k, 0:OWN, :] = frozen[:, 128 * k : 128 * (k + 1)]
        at_home = (me["z"] % 2, me["y"], core, me["x"], me["z"] // 2)
        loads[1].wait()
        dt_raw[at_home] = jnp.concatenate([down_t[...], jnp.zeros((RANK, 128 - OWN), BF16)], axis=1)

    def enter():
        pl.semaphore_wait(barrier, len(peers))

    def exchange():
        for n, (dx, dz) in enumerate(((1, 0), (0, 1), (1, 1))):
            tx, tz = (kx + dx) % 2, (kz + dz) % 2
            to = device(x=xq if dx else me["x"], z=zq if dz else me["z"])
            quad_copies.append(
                send(stage.at[tx * 2 + tz], quad.at[mine], quad_s.at[n], quad_r.at[n], to)
            )

    def piece():
        need(*quad_copies)
        quad[mine] = stage[mine]
        rows = jnp.concatenate([quad[k, 0:OWN, :].astype(F32) for k in range(4)], axis=0)
        w[kx, kz, me["z"] % 2, me["y"], core, me["x"] // 2] = rows.astype(BF16)

    def at_of(kind, at, r0, n):
        x, y, z, c = at["x"], at["y"], at["z"], at["core"]
        whole = lambda v: isinstance(v, slice)
        zhi, zlo = (ALL, ALL) if whole(z) else (z // 2, z % 2)
        rows = pl.ds(r0, n)
        if kind == "down":
            return dt_raw.at[zlo, y, c, x, zhi, rows, :]
        xhi, xlo = (ALL, ALL) if whole(x) else (x // 2, x % 2)
        return w.at[xlo, zhi, zlo, y, c, xhi, rows, :]

    done = set()

    def need(*copies):
        for copy in copies:
            if id(copy) not in done:
                done.add(id(copy))
                copy.wait_recv()

    class Stream:
        def __init__(self, name, n):
            self.n = n
            self.kind, (self.a, self.b, self.c), self.r0, self.rows = STREAMS[name]
            self.cut = self.rows // 32 * 16
            self.direct = name == "D"
            self.copies = {}
            self.sibs = {}

        def ref(self, at, part=None):
            r0, rows = self.r0, self.rows
            if part == 0:
                rows = self.cut
            elif part == 1:
                r0, rows = r0 + self.cut, rows - self.cut
            return at_of(self.kind, {**me, "core": core, **at}, r0, rows)

        def go(self, key, axis, by, at, part=None):
            ref = self.ref(at, part)
            n = len(self.copies)
            self.copies[key] = send(
                ref, ref, ag_s.at[self.n, n], ag_r.at[self.n, n], device(**{axis: step(axis, by)})
            )

        def sib(self, key, at):
            ref = self.ref(at)
            n = len(self.sibs)
            self.sibs[key] = send(ref, ref, sib_s.at[self.n, n], sib_r.at[self.n, n], sibling)

        def both(self, name, axis, at, k=""):
            at = {**at, axis: me[axis]}
            for end, by in (("P", side[axis]), ("O", -side[axis])):
                self.go(name + end + k, axis, by, at)

        def need_all(self, start):
            need(*(copy for key, copy in self.copies.items() if key[: len(start)] == start))

        def onward(self, name, end, axis, at):
            d = side[axis] if end == "P" else -side[axis]
            self.need_all(name + end)
            if self.direct and name == "2":
                return
            key = name + ("o" if end == "P" else "p")
            self.go(key, axis, -d, {**at, axis: step(axis, d)}, 0 if end == "P" else 1)

        def close(self, name):
            need(self.copies[name + "o"], self.copies[name + "p"])

        def sub(self, j):
            d = side[self.b]
            return {self.a: ALL, self.b: step(self.b, (0, d, -d, 2)[j])}

        def open1(self):
            for k in (1, 2, 3):
                self.go(f"1{k}", self.a, k, {})

        def row(self, k):
            if k:
                need(self.copies[f"1{k}"])
            return {self.a: step(self.a, -k)}

        def open2(self, k):
            self.both("2", self.b, self.row(k), str(k))
            if self.direct:
                self.go(f"2X{k}", self.b, 2, self.row(k))

        def open30(self, k):
            self.both("30", self.c, self.row(k), str(k))

        def close1(self):
            self.sib("20", self.sub(0))

        def fwd2(self, end):
            self.onward("2", end, self.b, {self.a: ALL})
            j = 1 if end == "P" else 2
            self.sib(f"2{j}", self.sub(j))

        def close2(self):
            if self.direct:
                self.need_all("2X")
            else:
                self.close("2")
            self.sib("23", self.sub(3))

        def open3(self, j):
            self.both(f"3{j}", self.c, self.sub(j))

        def fwd3(self, end, j):
            at = self.sub(j)
            self.onward(f"3{j}", end, self.c, at)
            d = side[self.c] if end == "P" else -side[self.c]
            self.sib(f"3{j}{end}", {**at, self.c: step(self.c, d)})

        def close3(self, j):
            self.close(f"3{j}")
            self.sib(f"3{j}o", {**self.sub(j), self.c: step(self.c, 2)})

        def need_sib(self, *keys):
            need(*(self.sibs[key] for key in keys))

    streams = {name: Stream(name, n) for n, name in enumerate(STREAMS)}

    x0_copies = {}
    state = {}

    def raised():
        loads[2].wait()
        loads[3].wait()
        loads[4].wait()
        first = (outer % 2 * 8 + inner) * ROWS
        position = first + lax.broadcasted_iota(jnp.int32, (ROWS, KV), 0)
        live = jnp.where(position < lengths[outer // 2], 1.0, 0.0).astype(BF16)
        masked[...] = cot[...] * live
        back = lax.dot_general(masked[...], up[...], CONTRACT, preferred_element_type=F32)
        state["raised2"] = back.astype(BF16) * jnp.asarray(adapter_scale, BF16)
        raised_out[...] = state["raised2"]
        state["raised2_t"] = state["raised2"].astype(F32).T.astype(BF16)
        total[...] = jnp.zeros_like(total)

    def owners(c):
        loads[5 + c].wait()
        for n in range(0, STEP, 256):
            m = min(256, STEP - n)
            g[:, n : n + m] = jnp.dot(
                state["raised2_t"], tokens[:, STEP * c + n : STEP * c + n + m], preferred_element_type=F32
            )
        for i in range(32):
            o, x, zhi = i // 8, i // 2 % 4, i % 2
            piece = g[:, OWN * i : OWN * (i + 1)]
            r[c // 2, 2 * (c % 2) + o // 2, o % 2, x, zhi, :, 0:OWN] = piece
            r[c // 2, 2 * (c % 2) + o // 2, o % 2, x, zhi, :, OWN:128] = jnp.zeros((RANK, 128 - OWN), F32)

    def owners_pair(c):
        zlo, y = c // 2, pl.ds(2 * (c % 2), 2)
        x0_copies[c] = send(r.at[zlo, y, 1 - core], x0.at[zlo, y], rs_s.at[0, c], rs_r.at[0, c], sibling)

    def add_sibling(c):
        need(x0_copies[c])
        for y in range(2 * (c % 2), 2 * (c % 2) + 2):
            for x in range(4):
                r[c // 2, y, core, x] = r[c // 2, y, core, x] + x0[c // 2, y, x]

    def r_at(at, r0, n):
        z = at["z"]
        zhi, zlo = (ALL, ALL) if isinstance(z, slice) else (z // 2, z % 2)
        return r.at[zlo, at["y"], core, at["x"], zhi, pl.ds(r0, n), :]

    class Sum:
        def __init__(self, n):
            self.n = n
            (self.a, self.b, self.c), self.r0, self.rows, self.cut = SUMS[n]
            self.free = {self.a: ALL, self.b: ALL, self.c: ALL}
            self.sends = []

        def go(self, src, dst, k, axis, by):
            copy = send(src, dst, rs_s.at[1 + self.n, k], rs_r.at[1 + self.n, k], device(**{axis: step(axis, by)}))
            self.sends.append(copy)
            return copy

        def at(self, by, half=None):
            r0, rows = self.r0, self.rows
            if half == 0:
                rows = self.cut
            elif half == 1:
                r0, rows = r0 + self.cut, rows - self.cut
            return r_at({**self.free, self.a: step(self.a, by)}, r0, rows)

        def pack(self, buffer, ref):
            buffer[...] = ref[...].reshape(buffer.shape).astype(BF16)
            return buffer

        def take(self, ref, buffer):
            ref[...] = ref[...] + buffer[...].astype(F32).reshape(ref.shape)

        def first(self):
            n = self.n
            self.ca = self.go(self.pack(sa[n], self.at(2, 0)), xa[n], 0, self.a, 1)
            self.cb = self.go(self.pack(sb[n], self.at(2, 1)), xb[n], 1, self.a, -1)

        def second(self):
            n = self.n
            need(self.ca)
            self.take(self.at(1, 0), xa[n])
            self.cl = self.go(self.pack(sl[n], self.at(1)), xl[n], 2, self.a, 1)
            need(self.cb)
            self.take(self.at(-1, 1), xb[n])
            self.cr = self.go(self.pack(sr[n], self.at(-1)), xr[n], 3, self.a, -1)

        def third(self):
            need(self.cl, self.cr)
            self.take(self.at(0), xl[self.n])
            self.take(self.at(0), xr[self.n])
            self.k = []
            for j, by in enumerate((1, -1, 2)):
                src = r_at({**self.free, self.a: me[self.a], self.b: step(self.b, by)}, self.r0, self.rows)
                out = self.pack(sy[self.n].at[j], src)
                self.k.append(self.go(out, y2[self.n].at[j], 4 + j, self.b, by))

        def fourth(self):
            need(*self.k)
            ref = r_at({**me, self.c: ALL}, self.r0, self.rows)
            for j in range(3):
                self.take(ref, y2[self.n].at[j])
            self.k = []
            for j, by in enumerate((1, -1, 2)):
                src = r_at({**me, self.c: step(self.c, by)}, self.r0, self.rows)
                self.k.append(self.go(src, y3[self.n].at[j], 7 + j, self.c, by))

        def fifth(self):
            need(*self.k)
            own = r_at(me, self.r0, self.rows)
            total = own[...] + y3[self.n][0] + y3[self.n][1] + y3[self.n][2]
            dgrad[self.r0 : self.r0 + self.rows, :] = total[:, 0:OWN]

    sums = [Sum(n) for n in range(3)]

    up_copies = []

    def up_send(src, dst, to):
        k = len(up_copies)
        copy = send(src, dst, up_s.at[k], up_r.at[k], to)
        up_copies.append(copy)
        return copy

    others = [(c, by) for c in range(2) for by in range(4) if (c, by) != (0, 0)]

    def up_rows(c, z):
        return pl.ds(pl.multiple_of(c * 32 + z * 8, 8), 8)

    def low_rows():
        down = streams["D"]
        down.need_sib(*down.sibs)
        for c in range(4):
            for i in range(32):
                o, x, zhi = i // 8, i // 2 % 4, i % 2
                piece = dt_raw[c // 2, 2 * (c % 2) + o // 2, o % 2, x, zhi]
                dt[:, OWN * i + STEP * c : OWN * (i + 1) + STEP * c] = piece[:, 0:OWN]

    def low(part):
        if part == 0:
            base, size = rows_of(me, 3, 1)
            at = pl.ds(pl.multiple_of(base, 128), size)
            dt_last[...] = dt[:, at]
            tokens_last[...] = tokens[:, at]
        first, last = (0, 8, 15, 22, 29)[part : part + 2]
        out = jnp.zeros((ROWS, RANK), F32) if part == 0 else low_sum[...]
        for c in range(first, last):
            out += lax.dot_general(
                tokens[:, 512 * c : 512 * (c + 1)], dt[:, 512 * c : 512 * (c + 1)], CONTRACT,
                preferred_element_type=F32,
            )
        if part < 3:
            low_sum[...] = out
            return
        lowered2 = out.astype(BF16) * jnp.asarray(adapter_scale, BF16)
        lowered2_t = lowered2.astype(F32).T.astype(BF16)
        u0[...] = jnp.dot(lowered2_t, masked[...], preferred_element_type=F32)
        state["k"] = []
        for j, (c, by) in enumerate(others):
            to_core, z = core + c - 2 * c * core, step("z", by)
            state["k"].append(up_send(u0.at[up_rows(to_core, z)], u1.at[j], device(core=to_core, z=z)))
        total[...] += jnp.dot(lowered2, up[...], preferred_element_type=F32)

    def wait_up():
        need(*state["k"])

    def up_x():
        wait_up()
        part = u0[up_rows(core, me["z"]), :]
        for j in range(len(others)):
            part = part + u1[j]
        u2[me["x"]] = part
        ref = u2.at[me["x"]]
        state["k"] = [up_send(ref, ref, device(x=step("x", by))) for by in (1, 2, 3)]

    def up_y():
        wait_up()
        u3[me["y"]] = u2[0] + u2[1] + u2[2] + u2[3]
        ref = u3.at[me["y"]]
        state["k"] = [up_send(ref, ref, device(y=step("y", by))) for by in (1, 2, 3)]

    def up_gather():
        wait_up()
        own = up_rows(core, me["z"])
        ugrad[own, :] = u3[0] + u3[1] + u3[2] + u3[3]
        ref = ugrad.at[own]
        state["k"] = [
            up_send(ref, ref, device(core=core + c - 2 * c * core, z=step("z", by))) for c, by in others
        ]

    w3 = w.reshape(4, D, 128)

    def arrived(j, zlo):
        streams["X"].need_sib(f"2{j}", *(f"3{j}{end}" for end in "POo"))
        streams["Z"].need_sib(*((f"2{j}", f"3{j}o") if zlo else (f"3{j}P", f"3{j}O")))
        subs = ((0, 3) if zlo else (1, 2)) if streams["Y"].b == "z" else range(4)
        streams["Y"].need_sib(*(f"3{i}{' POo'[j]}" if j else f"2{i}" for i in subs))

    def keys_part(j, zlo):
        arrived(j, zlo)
        at, wc = weights(w3, *rows_of(me, j, zlo))
        total[...] += jnp.dot(tokens[:, at], wc, preferred_element_type=F32)

    def last_rows():
        arrived(3, 1)
        at, _ = weights(w3, *rows_of(me, 3, 1))
        w_last[...] = w3[:, at, :]

    def input_part(j, zlo):
        base, size = rows_of(me, j, zlo)
        for n in range(0, size, 256):
            m = min(256, size - n)
            ig[:, pl.ds(pl.multiple_of(base + n, 128), m)] = input_columns(
                w3, dt, masked, state["raised2"], base + n, m
            )

    def add_siblings():
        for c in range(4):
            add_sibling(c)

    D_, Z_, X_, Y_ = streams.values()
    fill_stage()
    raised()
    owners(0)
    enter()
    owners_pair(0)
    D_.open1()
    D_.open2(0)
    exchange()
    owners(2)
    owners(3)
    owners_pair(3)
    owners_pair(2)
    owners(1)
    D_.open30(2)
    owners_pair(1)
    D_.open30(1)
    D_.open2(1)
    D_.open2(2)
    D_.open30(3)
    D_.open2(3)
    D_.close1()
    D_.open30(0)
    piece()
    Z_.open1()
    Y_.open1()
    Y_.open2(0)
    Y_.open30(0)
    Z_.open2(0)
    X_.open1()
    X_.open2(0)
    Z_.open30(0)
    X_.open30(0)
    add_siblings()
    sums[1].first()
    sums[2].first()
    sums[0].first()
    D_.fwd3("P", 0)
    D_.fwd3("O", 0)
    D_.fwd2("P")
    D_.fwd2("O")
    D_.open3(2)
    D_.open3(1)
    Y_.open2(1)
    Y_.open30(1)
    Y_.open2(2)
    Y_.open30(2)
    D_.close2()
    D_.open3(3)
    Z_.open2(1)
    Z_.open2(2)
    Y_.open30(3)
    Y_.open2(3)
    Y_.close1()
    X_.open2(1)
    X_.open2(2)
    X_.open30(1)
    X_.open30(2)
    Z_.open2(3)
    Z_.close1()
    Z_.open30(2)
    X_.open2(3)
    X_.open30(3)
    X_.close1()
    Z_.open30(3)
    sums[2].second()
    sums[1].second()
    D_.close3(0)
    sums[0].second()
    Y_.fwd2("P")
    Z_.open30(1)
    D_.fwd3("P", 2)
    D_.fwd3("O", 2)
    Y_.fwd3("O", 0)
    Y_.fwd2("O")
    Y_.fwd3("P", 0)
    D_.fwd3("P", 1)
    D_.fwd3("O", 1)
    Y_.open3(1)
    X_.fwd3("P", 0)
    D_.fwd3("P", 3)
    D_.fwd3("O", 3)
    Z_.fwd2("O")
    X_.fwd3("O", 0)
    Z_.fwd2("P")
    Z_.open3(1)
    X_.fwd2("O")
    X_.fwd2("P")
    X_.open3(1)
    sums[0].third()
    X_.open3(2)
    sums[2].third()
    Z_.open3(2)
    Y_.close2()
    sums[1].third()
    Z_.fwd3("P", 0)
    Z_.fwd3("O", 0)
    D_.close3(2)
    Y_.close3(0)
    D_.close3(1)
    X_.close3(0)
    Y_.open3(2)
    D_.close3(3)
    Y_.fwd3("O", 1)
    keys_part(0, 0)
    Y_.fwd3("P", 1)
    low_rows()
    low(0)
    X_.fwd3("P", 1)
    low(1)
    X_.fwd3("O", 1)
    Y_.open3(3)
    low(2)
    low(3)
    Z_.fwd3("P", 1)
    Z_.fwd3("O", 1)
    X_.close2()
    X_.open3(3)
    Z_.close2()
    input_part(0, 0)
    X_.fwd3("P", 2)
    Z_.open3(3)
    sums[0].fourth()
    X_.fwd3("O", 2)
    Z_.fwd3("P", 2)
    Z_.fwd3("O", 2)
    Y_.fwd3("O", 2)
    sums[2].fourth()
    Y_.fwd3("P", 2)
    sums[1].fourth()
    X_.close3(1)
    Y_.close3(1)
    Z_.close3(0)
    Y_.fwd3("O", 3)
    up_x()
    keys_part(0, 1)
    Y_.fwd3("P", 3)
    X_.fwd3("P", 3)
    input_part(0, 1)
    Z_.close3(1)
    X_.fwd3("O", 3)
    keys_part(1, 0)
    sums[2].fifth()
    input_part(1, 0)
    X_.close3(2)
    keys_part(1, 1)
    sums[1].fifth()
    up_y()
    Z_.fwd3("O", 3)
    Z_.fwd3("P", 3)
    input_part(1, 1)
    keys_part(2, 0)
    X_.close3(3)
    Z_.close3(2)
    sums[0].fifth()
    input_part(2, 0)
    Y_.close3(2)
    Y_.close3(3)
    up_gather()
    keys_part(2, 1)
    input_part(2, 1)
    Z_.close3(3)
    keys_part(3, 0)
    input_part(3, 0)
    last_rows()
    wait_up()
    for s in streams.values():
        need(*s.copies.values(), *s.sibs.values())
    for copy in sent:
        left(copy)


def last_kernel(
    ig, total, dgrad, ugrad, w, dt, tokens, masked, raised2,
    keys_hbm, ig_hbm, dgrad_hbm, ugrad_hbm,
    last, keys, sem,
):
    outer, inner = lax.axis_index("outer"), lax.axis_index("inner")
    me = place(outer, inner)
    copies = []

    def store(src, dst):
        copies.append(pltpu.make_async_copy(src, dst, sem.at[len(copies)]))
        copies[-1].start()

    zlo, pair = me["z"] % 2, me["y"] // 2
    early, early_size = rows_of(me, 2, 1)
    for base, size in (
        ((1 - zlo) * 7424, 7424), (zlo * 7424 + pair * STEP, STEP), (early, early_size)
    ):
        at = pl.ds(pl.multiple_of(base, 128), size)
        store(ig.at[:, at], ig_hbm.at[:, at])
    store(dgrad, dgrad_hbm)
    store(ugrad, ugrad_hbm)
    base, size = rows_of(me, 3, 1)
    for n in range(0, size, 640):
        for k in range(n, n + 640, 256):
            m = min(256, n + 640 - k)
            last[:, k : k + m] = input_columns(w, dt, masked, raised2[...], k, m)
        at = pl.ds(pl.multiple_of(base + n, 128), 640)
        store(last.at[:, n : n + 640], ig_hbm.at[:, at])
    _, wc = weights(w, 0, size)
    out = total[...] + jnp.dot(tokens[...], wc, preferred_element_type=F32)
    keys[...] = out.astype(BF16)
    store(keys, keys_hbm)
    for copy in copies:
        copy.wait()


def on_device(tokens, cotangent, lengths, frozen, down_weight, up_weight):
    vmem = pl.BlockSpec(memory_space=pltpu.VMEM)
    anywhere = pl.BlockSpec(memory_space=pl.ANY)
    in_hbm = lambda array: pltpu.with_memory_space_constraint(array, pltpu.HBM)
    down_t = down_weight.T
    def halves(rows):
        return [pltpu.VMEM((16 * rows(n), 128), BF16) for n in range(3)]

    def fours():
        return [pltpu.VMEM((3, 4 * SUMS[n][2], 128), BF16) for n in range(3)]

    def buffers(shape):
        return [pltpu.VMEM(shape(n), F32) for n in range(3)]

    scratch = [
        pltpu.VMEM((2, 2, 2, 4, 2, 2, QUAD, 128), BF16),
        pltpu.VMEM((RANK, D), BF16),
        pltpu.VMEM((ROWS, D), BF16),
        pltpu.SMEM((8,), jnp.int32),
        pltpu.VMEM((ROWS, KV), BF16),
        pltpu.VMEM((OWN, KV), BF16),
        pltpu.VMEM((RANK, OWN), BF16),
        pltpu.VMEM((RANK, KV), BF16),
        pltpu.VMEM((4, 128, 128), BF16),
        pltpu.VMEM((4, 128, 128), BF16),
        pltpu.VMEM((2, 4, 2, 4, 2, RANK, 128), BF16),
        pltpu.VMEM((RANK, STEP), F32),
        pltpu.VMEM((2, 4, 2, 4, 2, RANK, 128), F32),
        pltpu.VMEM((2, 4, 4, 2, RANK, 128), F32),
        *[halves(lambda n: SUMS[n][3]), halves(lambda n: SUMS[n][2] - SUMS[n][3])],
        *[halves(lambda n: SUMS[n][2]) for _ in range(2)],
        fours(),
        *[halves(lambda n: SUMS[n][3]), halves(lambda n: SUMS[n][2] - SUMS[n][3])],
        *[halves(lambda n: SUMS[n][2]) for _ in range(2)],
        fours(),
        buffers(lambda n: (3, SUMS[n][2], 128)),
        pltpu.VMEM((RANK, KV), F32),
        pltpu.VMEM((7, 8, KV), F32),
        pltpu.VMEM((4, 8, KV), F32),
        pltpu.VMEM((4, 8, KV), F32),
        pltpu.VMEM((ROWS, RANK), F32),
        pltpu.SemaphoreType.DMA((9,)),
        pltpu.SemaphoreType.DMA((3,)),
        pltpu.SemaphoreType.DMA((3,)),
        pltpu.SemaphoreType.DMA((4, 40)),
        pltpu.SemaphoreType.DMA((4, 40)),
        pltpu.SemaphoreType.DMA((4, 16)),
        pltpu.SemaphoreType.DMA((4, 16)),
        pltpu.SemaphoreType.DMA((4, 10)),
        pltpu.SemaphoreType.DMA((4, 10)),
        pltpu.SemaphoreType.DMA((20,)),
        pltpu.SemaphoreType.DMA((20,)),
    ]
    grads = [((RANK, OWN), F32), ((RANK, KV), F32)]
    shapes = [((ROWS, D), BF16), ((ROWS, KV), F32)] + grads
    shapes += [((4, 1920, 128), BF16), ((RANK, 1920), BF16), ((ROWS, 1920), BF16)]
    shapes += [((ROWS, KV), BF16), ((ROWS, RANK), BF16)]
    inputs = (lengths, tokens, cotangent, frozen, down_t, up_weight)
    results = pl.pallas_call(
        comm_kernel,
        out_shape=tuple(pltpu.VMEM(*shape) for shape in shapes),
        in_specs=[anywhere] * 6,
        out_specs=(vmem,) * len(shapes),
        scratch_shapes=scratch,
        compiler_params=pltpu.CompilerParams(
            collective_id=0, has_side_effects=True, vmem_limit_bytes=46 * 1024 * 1024
        ),
        name="gather_multiply_sum",
    )(*[in_hbm(array) for array in inputs])
    results = [pltpu.with_memory_space_constraint(array, pltpu.VMEM) for array in results]
    outs = [((ROWS, KV), BF16), ((ROWS, D), BF16)] + grads
    keys, ig, dgrad, ugrad = pl.pallas_call(
        last_kernel,
        out_shape=tuple(jax.ShapeDtypeStruct(*shape) for shape in outs),
        in_specs=[vmem] * len(results),
        out_specs=(anywhere,) * 4,
        scratch_shapes=[
            pltpu.VMEM((ROWS, 1920), BF16),
            pltpu.VMEM((ROWS, KV), BF16),
            pltpu.SemaphoreType.DMA((9,)),
        ],
        compiler_params=pltpu.CompilerParams(vmem_limit_bytes=8 * 1024 * 1024),
        name="last_products",
    )(*results)
    return keys, ig, dgrad.T, ugrad


def solution(mesh):
    return jax.shard_map(
        on_device,
        mesh=mesh,
        in_specs=(
            P(("outer", "inner"), None),
            P(("outer", "inner"), None),
            P(),
            P(("outer", "inner"), None),
            P(("outer", "inner"), None),
            P(),
        ),
        out_specs=(
            P(("outer", "inner"), None),
            P(("outer", "inner"), None),
            P(("outer", "inner"), None),
            P(),
        ),
        check_vma=False,
    )
```
